32 devices in a mesh: gx: 4 (over x, core), gy: 2 (over y), sa: 4 (over z).
Axes of the slice: x: 2, y: 2, z: 4, core: 2. Of those that a mesh axis runs over, the one named last changes fastest.
Arguments:
- green: bfloat16 [8, 4, 2, 2, 1024, 256], P('gx', 'gy', None, None, 'sa'), may hold values from -0.59765625 to 0.59765625
- offsets: int32 [4, 2], replicated, may hold values from -1 to 1, as said below
Outputs:
- hessian: float32 [8, 4, 4, 2, 256, 512], P('gx', 'gy', None, None, 'sa')
The draws below stay inside these ranges and needn't reach their ends.
Inputs may be any that keep to these rules, and one draw needn't show every extreme that they name: `offsets`: each row is an offset (dx, dy) within 1 tiles with dx >= 0, and dy >= 0 where dx = 0; rows are distinct; (1, -1) and (1, 1) are always among them.
All inputs are finite; a program needn't handle non-finite values.
Results may differ from the reference program's by a relative error of at most 0.0003.
Values may be sent and summed in bfloat16 or wider, within the bound.
A program may use at most 128 MiB of HBM per device.

```python
import jax
import jax.numpy as jnp
from jax import lax

P_SIZE = 256
NF = 2
NPAIR = 4
TILES_X = 8
TILES_Y = 4
S = 1024


def draw_offsets(key, part):
    key = jax.random.fold_in(key, 7)
    loose = jnp.array([[0, 0], [0, 1], [1, 0]], jnp.int32)
    forced = jnp.array([[1, -1], [1, 1]], jnp.int32)
    picked = jax.random.permutation(key, 3)[:2]
    rows = jnp.concatenate([loose[picked], forced], axis=0)
    order = jax.random.permutation(jax.random.fold_in(key, 1), 4)
    return rows[order]


def level_of(stream_key, dims, cuts, least, top_value):
    def one(position, shards_of):
        draws = jax.random.uniform(jax.random.fold_in(jax.random.fold_in(stream_key, 6), position), (shards_of,), jnp.float32, least / len(cuts), top_value / len(cuts))
        return jnp.repeat(jnp.exp(draws), dims[position] // shards_of).reshape((-1,) + (1,) * (len(dims) - position - 1))

    factor_of = one(*cuts[0])
    for cut in cuts[1:]:
        factor_of = factor_of * one(*cut)
    return factor_of


def scatter_about(own_key, dims, spread, most, cuts=(), kind=jnp.bfloat16):
    gain = level_of(own_key, dims, cuts, -0.22, 0.18) if cuts else 1.0
    values = jax.random.normal(own_key, dims, jnp.float32) * spread * gain
    return jnp.minimum(jnp.maximum(values, -most), most).astype(kind)


def setup_inputs(seed: int = 0) -> dict:
    splits = jax.random.split(jax.random.key(seed), 3)
    green = scatter_about(splits[0], (TILES_X, TILES_Y, NF, 2, S, P_SIZE), 0.1, 0.59765625, ((0, 4), (1, 2), (4, 4)))
    offsets = draw_offsets(jax.random.fold_in(splits[2], 71), 0)
    return {"green": green, "offsets": offsets}


def pair_block(left, right):
    return lax.dot_general(left, right, (((0,), (0,)), ((), ())), preferred_element_type=jnp.float32)


def reference(green, offsets):
    padded = jnp.pad(green, ((1, 1), (1, 1), (0, 0), (0, 0), (0, 0), (0, 0)))
    zero = jnp.int32(0)

    def one_tile(flat):
        flat = flat.astype(jnp.int32)
        pos_x = flat // TILES_Y
        pos_y = flat % TILES_Y
        own = lax.dynamic_slice(green, (pos_x, pos_y, zero, zero, zero, zero), (1, 1, NF, 2, S, P_SIZE))
        left = own.reshape(NF, 2 * S, P_SIZE)
        blocks = []
        for index in range(NPAIR):
            start_x = (pos_x + 1 + offsets[index, 0]).astype(jnp.int32)
            start_y = (pos_y + 1 + offsets[index, 1]).astype(jnp.int32)
            beside = lax.dynamic_slice(padded, (start_x, start_y, zero, zero, zero, zero), (1, 1, NF, 2, S, P_SIZE))
            beside = beside.reshape(NF, 2, S, P_SIZE)
            real_rows = beside.reshape(NF, 2 * S, P_SIZE)
            imag_rows = jnp.concatenate([beside[:, 1], -beside[:, 0]], axis=1)
            right = jnp.concatenate([real_rows, imag_rows], axis=2)
            freq_blocks = [pair_block(left[freq], right[freq]) for freq in range(NF)]
            blocks.append(jnp.stack(freq_blocks, axis=0))
        return jnp.stack(blocks, axis=0)

    result = lax.map(one_tile, jnp.arange(TILES_X * TILES_Y, dtype=jnp.int32))
    return result.reshape(TILES_X, TILES_Y, NPAIR, NF, P_SIZE, 2 * P_SIZE)
```

```python
import functools

import jax
import jax.numpy as jnp
from jax import lax
from jax.experimental import pallas as pl
from jax.experimental.pallas import tpu as pltpu
from jax.sharding import PartitionSpec as P

MESH = pl.DeviceIdType.MESH
CANDIDATES = ((0, 0), (0, 1), (1, -1), (1, 0), (1, 1))


def kernel(
    nx, ny, nz, green, out, own, up, down, right, turned, left,
    load_sem, own_sem, up_sem, down_sem, right_sem,
    send_zu, send_zd, send_yu, send_yd, send_x,
):
    tiles_x, tiles_y, freqs, _, _, traces, points = own.shape
    width = points // nz
    chunks = tiles_x * tiles_y * freqs
    gx, gy, gz = lax.axis_index("gx"), lax.axis_index("gy"), lax.axis_index("sa")
    has_right, has_left = gx < nx - 1, gx > 0
    has_up, has_down = gy < ny - 1, gy > 0
    has_above, has_below = gz < nz - 1, gz > 0

    def split(j):
        return j // (tiles_y * freqs), (j // freqs) % tiles_y, j % freqs

    def chunk(slab, j):
        tx, ty, f = split(j)
        return own.at[tx, ty, f, slab]

    def load(j):
        tx, ty, f = split(j)
        return pltpu.make_async_copy(green.at[tx, ty, f], own.at[tx, ty, f, gz], load_sem.at[j])

    def remote(src, dst, send, recv, **where):
        return pltpu.make_async_remote_copy(
            src_ref=src, dst_ref=dst, send_sem=send, recv_sem=recv, device_id=where, device_id_type=MESH
        )

    def z_up(slab, j):
        here = chunk(slab, j)
        return remote(here, here, send_zu.at[slab, j], own_sem.at[slab, j], sa=gz + 1)

    def z_down(slab, j):
        here = chunk(slab, j)
        return remote(here, here, send_zd.at[slab, j], own_sem.at[slab, j], sa=gz - 1)

    def y_down(slab, tx, f):
        return remote(
            own.at[tx, 0, f, slab], up.at[tx, f, slab],
            send_yd.at[slab, tx, f], up_sem.at[slab, tx, f], gy=gy - 1,
        )

    def y_up(slab, tx, f):
        return remote(
            own.at[tx, tiles_y - 1, f, slab], down.at[tx, f, slab],
            send_yu.at[slab, tx, f], down_sem.at[slab, tx, f], gy=gy + 1,
        )

    def x_left(src, slab, row, f):
        return remote(
            src, right.at[row, f, slab], send_x.at[slab, row, f], right_sem.at[slab, row, f], gx=gx - 1
        )

    def each(count, body):
        def step(i, carry):
            body(i)
            return carry

        lax.fori_loop(0, count, step, 0)

    each(chunks, lambda j: load(j).start())

    barrier = pltpu.get_barrier_semaphore()
    sides = (
        (has_above, dict(sa=gz + 1)), (has_below, dict(sa=gz - 1)),
        (has_up, dict(gy=gy + 1)), (has_down, dict(gy=gy - 1)),
        (has_right, dict(gx=gx + 1)), (has_left, dict(gx=gx - 1)),
    )
    for there, where in sides:
        @pl.when(there)
        def _():
            pl.semaphore_signal(barrier, inc=1, device_id=where, device_id_type=MESH)
    pl.semaphore_wait(barrier, sum(there.astype(jnp.int32) for there, _ in sides))

    def pass_on(slab, j, upward, downward):
        tx, ty, f = split(j)
        if upward:
            pl.when(has_above)(lambda: z_up(slab, j).start())
        if downward:
            pl.when(has_below)(lambda: z_down(slab, j).start())
        pl.when((ty == 0) & has_down)(lambda: y_down(slab, tx, f).start())
        pl.when((ty == tiles_y - 1) & has_up)(lambda: y_up(slab, tx, f).start())
        pl.when((tx == 0) & has_left)(
            lambda: x_left(own.at[0, ty, f, slab], slab, ty + 1, f).start()
        )

    def halo(slab):
        def body(i):
            tx, f = i // freqs, i % freqs

            @pl.when(has_up)
            def _():
                y_down(slab, tx, f).wait_recv()
                pl.when((tx == 0) & has_left)(
                    lambda: x_left(up.at[0, f, slab], slab, tiles_y + 1, f).start()
                )

            @pl.when(has_down)
            def _():
                y_up(slab, tx, f).wait_recv()
                pl.when((tx == 0) & has_left)(
                    lambda: x_left(down.at[0, f, slab], slab, 0, f).start()
                )

        each(tiles_x * freqs, body)

        @pl.when(has_right)
        def _():
            def arrive(i):
                row, f = i // freqs, i % freqs

                def wait():
                    x_left(right.at[row, f, slab], slab, row, f).wait_recv()

                pl.when(((row > 0) | has_down) & ((row < tiles_y + 1) | has_up))(wait)

            each((tiles_y + 2) * freqs, arrive)

    lane = pl.multiple_of(gz * width // 128 * 128, 128)
    row_at = pl.multiple_of(gz * width % 128, width)

    def products(slab):
        def at_frequency(f):
            for tx in range(tiles_x):
                for ty in range(tiles_y):
                    for part in range(2):
                        turned[part] = own[tx, ty, f, slab, part, :, pl.ds(lane, 128)].T
                    real = turned[0, pl.ds(row_at, width), :]
                    imag = turned[1, pl.ds(row_at, width), :]
                    left[:width, :traces] = real
                    left[:width, traces:] = imag
                    left[width:, :traces] = -imag
                    left[width:, traces:] = real
                    for c, (dx, dy) in enumerate(CANDIDATES):
                        ox, oy = tx + dx, ty + dy
                        there = True
                        if ox == tiles_x:
                            there = has_right
                            beside = right.at[oy + 1, f, slab]
                        elif oy == tiles_y:
                            beside = up.at[ox, f, slab]
                        elif oy < 0:
                            beside = down.at[ox, f, slab]
                        else:
                            beside = own.at[ox, oy, f, slab]
                        if oy == tiles_y:
                            there = there & has_up
                        if oy < 0:
                            there = there & has_down

                        def add(beside=beside, c=c):
                            block = jnp.dot(
                                left[...], beside[...].reshape(2 * traces, points),
                                preferred_element_type=jnp.float32,
                            )
                            out[tx, ty, c, f, :, :points] += block[:width]
                            out[tx, ty, c, f, :, points:] += block[width:]

                        if there is True:
                            add()
                        else:
                            pl.when(there)(add)

        each(freqs, at_frequency)

    out[...] = jnp.zeros_like(out)

    for d in range(nz):
        if d == 0:
            def begin(j):
                load(j).wait()
                pass_on(gz, j, True, True)

            each(chunks, begin)
            halo(gz)
            products(gz)
        else:
            lower, upper = gz - d, gz + d

            def arrive(j):
                @pl.when(lower >= 0)
                def _():
                    z_up(lower, j).wait_recv()
                    pass_on(lower, j, True, False)

                @pl.when(upper < nz)
                def _():
                    z_down(upper, j).wait_recv()
                    pass_on(upper, j, False, True)

            each(chunks, arrive)
            for valid, slab in ((lower >= 0, lower), (upper < nz, upper)):
                @pl.when(valid)
                def _():
                    halo(slab)
                    products(slab)

    def finish(slab):
        def body(j):
            tx, ty, f = split(j)
            pl.when(has_above & (slab <= gz))(lambda: z_up(slab, j).wait_send())
            pl.when(has_below & (slab >= gz))(lambda: z_down(slab, j).wait_send())
            pl.when((ty == 0) & has_down)(lambda: y_down(slab, tx, f).wait_send())
            pl.when((ty == tiles_y - 1) & has_up)(lambda: y_up(slab, tx, f).wait_send())
            pl.when((tx == 0) & has_left)(
                lambda: x_left(own.at[0, ty, f, slab], slab, ty + 1, f).wait_send()
            )

        each(chunks, body)

        def edges(f):
            pl.when(has_up & has_left)(
                lambda: x_left(up.at[0, f, slab], slab, tiles_y + 1, f).wait_send()
            )
            pl.when(has_down & has_left)(
                lambda: x_left(down.at[0, f, slab], slab, 0, f).wait_send()
            )

        each(freqs, edges)

    each(nz, finish)


def per_device(green, offsets):
    tiles_x, tiles_y, freqs, _, traces, points = green.shape
    nx, ny, nz = (lax.axis_size(name) for name in ("gx", "gy", "sa"))
    width = points // nz
    chunks = tiles_x * tiles_y * freqs
    slabs = (nz, 2, traces, points)
    dma = pltpu.SemaphoreType.DMA
    blocks = pl.pallas_call(
        functools.partial(kernel, nx, ny, nz),
        out_shape=jax.ShapeDtypeStruct(
            (tiles_x, tiles_y, len(CANDIDATES), freqs, width, 2 * points), jnp.float32
        ),
        in_specs=[pl.BlockSpec(memory_space=pl.ANY)],
        out_specs=pl.BlockSpec(memory_space=pltpu.VMEM),
        scratch_shapes=[
            pltpu.VMEM((tiles_x, tiles_y, freqs) + slabs, jnp.bfloat16),
            pltpu.VMEM((tiles_x, freqs) + slabs, jnp.bfloat16),
            pltpu.VMEM((tiles_x, freqs) + slabs, jnp.bfloat16),
            pltpu.VMEM((tiles_y + 2, freqs) + slabs, jnp.bfloat16),
            pltpu.VMEM((2, 128, traces), jnp.bfloat16),
            pltpu.VMEM((2 * width, 2 * traces), jnp.bfloat16),
            dma((chunks,)),
            dma((nz, chunks)),
            dma((nz, tiles_x, freqs)),
            dma((nz, tiles_x, freqs)),
            dma((nz, tiles_y + 2, freqs)),
            dma((nz, chunks)),
            dma((nz, chunks)),
            dma((nz, tiles_x, freqs)),
            dma((nz, tiles_x, freqs)),
            dma((nz, tiles_y + 2, freqs)),
        ],
        compiler_params=pltpu.CompilerParams(
            collective_id=0, has_side_effects=True, vmem_limit_bytes=58 * 2**20
        ),
        cost_estimate=pl.CostEstimate(
            flops=2 * chunks * len(CANDIDATES) * width * 2 * points * 2 * traces * nz,
            bytes_accessed=12 * 2**20, transcendentals=0,
        ),
    )(green)
    dx, dy = offsets[:, 0], offsets[:, 1]
    wanted = jnp.where(dx == 0, dy, dy + 3)
    return jnp.stack(
        [lax.dynamic_index_in_dim(blocks, wanted[k], 2, keepdims=False) for k in range(offsets.shape[0])],
        axis=2,
    )


def solution(mesh):
    return jax.shard_map(
        per_device,
        mesh=mesh,
        in_specs=(P("gx", "gy", None, None, "sa", None), P()),
        out_specs=P("gx", "gy", None, None, "sa", None),
        check_vma=False,
    )
```

```python
import functools

import jax
import jax.numpy as jnp
from jax import lax
from jax.experimental import pallas as pl
from jax.experimental.pallas import tpu as pltpu
from jax.sharding import PartitionSpec as P

MESH = pl.DeviceIdType.MESH
CANDIDATES = ((0, 0), (0, 1), (1, -1), (1, 0), (1, 1))


def kernel(
    nx, ny, nz, green, offsets, out, total, own, up, down, right, turned, left,
    load_sem, own_sem, up_sem, down_sem, right_sem,
    send_zu, send_zd, send_yu, send_yd, send_x,
):
    tiles_x, tiles_y, freqs, _, _, traces, points = own.shape
    width = points // nz
    tiles = tiles_x * tiles_y
    chunks = tiles * freqs
    gx, gy, gz = lax.axis_index("gx"), lax.axis_index("gy"), lax.axis_index("sa")
    has_right, has_left = gx < nx - 1, gx > 0
    has_up, has_down = gy < ny - 1, gy > 0
    has_above, has_below = gz < nz - 1, gz > 0

    def split(j):
        return (j // tiles_y) % tiles_x, j % tiles_y, j // tiles

    def chunk(slab, j):
        tx, ty, f = split(j)
        return own.at[tx, ty, f, slab]

    def load(j):
        tx, ty, f = split(j)
        return pltpu.make_async_copy(green.at[tx, ty, f], own.at[tx, ty, f, gz], load_sem.at[j])

    def remote(src, dst, send, recv, **where):
        return pltpu.make_async_remote_copy(
            src_ref=src, dst_ref=dst, send_sem=send, recv_sem=recv, device_id=where, device_id_type=MESH
        )

    def z_up(slab, j):
        here = chunk(slab, j)
        return remote(here, here, send_zu.at[slab, j], own_sem.at[slab, j], sa=gz + 1)

    def z_down(slab, j):
        here = chunk(slab, j)
        return remote(here, here, send_zd.at[slab, j], own_sem.at[slab, j], sa=gz - 1)

    def y_down(slab, tx, f):
        return remote(
            own.at[tx, 0, f, slab], up.at[tx, f, slab],
            send_yd.at[slab, tx, f], up_sem.at[slab, tx, f], gy=gy - 1,
        )

    def y_up(slab, tx, f):
        return remote(
            own.at[tx, tiles_y - 1, f, slab], down.at[tx, f, slab],
            send_yu.at[slab, tx, f], down_sem.at[slab, tx, f], gy=gy + 1,
        )

    def x_left(src, slab, row, f):
        return remote(
            src, right.at[row, f, slab], send_x.at[slab, row, f], right_sem.at[slab, row, f], gx=gx - 1
        )

    def each(count, body, start=0):
        def step(i, carry):
            body(i)
            return carry

        lax.fori_loop(start, start + count, step, 0)

    each(chunks, lambda j: load(j).start())

    barrier = pltpu.get_barrier_semaphore()
    sides = (
        (has_above, dict(sa=gz + 1)), (has_below, dict(sa=gz - 1)),
        (has_up, dict(gy=gy + 1)), (has_down, dict(gy=gy - 1)),
        (has_right, dict(gx=gx + 1)), (has_left, dict(gx=gx - 1)),
    )
    for there, where in sides:
        @pl.when(there)
        def _():
            pl.semaphore_signal(barrier, inc=1, device_id=where, device_id_type=MESH)
    pl.semaphore_wait(barrier, sum(there.astype(jnp.int32) for there, _ in sides))

    def pass_on(slab, j, upward, downward):
        tx, ty, f = split(j)
        if upward:
            pl.when(has_above)(lambda: z_up(slab, j).start())
        if downward:
            pl.when(has_below)(lambda: z_down(slab, j).start())
        pl.when((ty == 0) & has_down)(lambda: y_down(slab, tx, f).start())
        pl.when((ty == tiles_y - 1) & has_up)(lambda: y_up(slab, tx, f).start())
        pl.when((tx == 0) & has_left)(
            lambda: x_left(own.at[0, ty, f, slab], slab, ty + 1, f).start()
        )

    def halo(slab, f):
        def body(tx):
            @pl.when(has_up)
            def _():
                y_down(slab, tx, f).wait_recv()
                pl.when((tx == 0) & has_left)(
                    lambda: x_left(up.at[0, f, slab], slab, tiles_y + 1, f).start()
                )

            @pl.when(has_down)
            def _():
                y_up(slab, tx, f).wait_recv()
                pl.when((tx == 0) & has_left)(
                    lambda: x_left(down.at[0, f, slab], slab, 0, f).start()
                )

        each(tiles_x, body)

        @pl.when(has_right)
        def _():
            def arrive(row):
                def wait():
                    x_left(right.at[row, f, slab], slab, row, f).wait_recv()

                pl.when(((row > 0) | has_down) & ((row < tiles_y + 1) | has_up))(wait)

            each(tiles_y + 2, arrive)

    lane = pl.multiple_of(gz * width // 128 * 128, 128)
    row_at = pl.multiple_of(gz * width % 128, width)

    def products(slab, f):
        for tx in range(tiles_x):
            for ty in range(tiles_y):
                for part in range(2):
                    turned[part] = own[tx, ty, f, slab, part, :, pl.ds(lane, 128)].T
                real = turned[0, pl.ds(row_at, width), :]
                imag = turned[1, pl.ds(row_at, width), :]
                left[:width, :traces] = real
                left[:width, traces:] = imag
                left[width:, :traces] = -imag
                left[width:, traces:] = real
                for c, (dx, dy) in enumerate(CANDIDATES):
                    ox, oy = tx + dx, ty + dy
                    there = True
                    if ox == tiles_x:
                        there = has_right
                        beside = right.at[oy + 1, f, slab]
                    elif oy == tiles_y:
                        beside = up.at[ox, f, slab]
                    elif oy < 0:
                        beside = down.at[ox, f, slab]
                    else:
                        beside = own.at[ox, oy, f, slab]
                    if oy == tiles_y:
                        there = there & has_up
                    if oy < 0:
                        there = there & has_down

                    def add(beside=beside, c=c):
                        block = jnp.dot(
                            left[...], beside[...].reshape(2 * traces, points),
                            preferred_element_type=jnp.float32,
                        )
                        total[tx, ty, c, f, :, :points] += block[:width]
                        total[tx, ty, c, f, :, points:] += block[width:]

                    if there is True:
                        add()
                    else:
                        pl.when(there)(add)

    def select(f):
        for k in range(offsets.shape[1]):
            wanted = offsets[1, k] + 3 * offsets[0, k]
            for tx in range(tiles_x):
                for ty in range(tiles_y):
                    out[tx, ty, k, f] = total[tx, ty, wanted, f]

    total[...] = jnp.zeros_like(total)

    def take_own(f):
        def begin(j):
            load(j).wait()
            pass_on(gz, j, True, True)

        each(tiles, begin, f * tiles)

    each(freqs, take_own)

    def own_part(f):
        halo(gz, f)
        products(gz, f)

    each(freqs, own_part)

    for d in range(1, nz):
        lower, upper = gz - d, gz + d

        def further(f):
            def arrive(j):
                @pl.when(lower >= 0)
                def _():
                    z_up(lower, j).wait_recv()
                    pass_on(lower, j, True, False)

                @pl.when(upper < nz)
                def _():
                    z_down(upper, j).wait_recv()
                    pass_on(upper, j, False, True)

            each(tiles, arrive, f * tiles)
            for valid, slab in ((lower >= 0, lower), (upper < nz, upper)):
                @pl.when(valid)
                def _():
                    halo(slab, f)
                    products(slab, f)

            if d == nz - 1:
                select(f)

        each(freqs, further)

    def finish(slab):
        def body(j):
            tx, ty, f = split(j)
            pl.when(has_above & (slab <= gz))(lambda: z_up(slab, j).wait_send())
            pl.when(has_below & (slab >= gz))(lambda: z_down(slab, j).wait_send())
            pl.when((ty == 0) & has_down)(lambda: y_down(slab, tx, f).wait_send())
            pl.when((ty == tiles_y - 1) & has_up)(lambda: y_up(slab, tx, f).wait_send())
            pl.when((tx == 0) & has_left)(
                lambda: x_left(own.at[0, ty, f, slab], slab, ty + 1, f).wait_send()
            )

        each(chunks, body)

        def edges(f):
            pl.when(has_up & has_left)(
                lambda: x_left(up.at[0, f, slab], slab, tiles_y + 1, f).wait_send()
            )
            pl.when(has_down & has_left)(
                lambda: x_left(down.at[0, f, slab], slab, 0, f).wait_send()
            )

        each(freqs, edges)

    each(nz, finish)


def per_device(green, offsets):
    tiles_x, tiles_y, freqs, _, traces, points = green.shape
    nx, ny, nz = (lax.axis_size(name) for name in ("gx", "gy", "sa"))
    width = points // nz
    chunks = tiles_x * tiles_y * freqs
    slabs = (nz, 2, traces, points)
    dma = pltpu.SemaphoreType.DMA
    return pl.pallas_call(
        functools.partial(kernel, nx, ny, nz),
        out_shape=jax.ShapeDtypeStruct(
            (tiles_x, tiles_y, offsets.shape[0], freqs, width, 2 * points), jnp.float32
        ),
        in_specs=[pl.BlockSpec(memory_space=pl.ANY), pl.BlockSpec(memory_space=pltpu.SMEM)],
        out_specs=pl.BlockSpec(memory_space=pltpu.VMEM),
        scratch_shapes=[
            pltpu.VMEM(
                (tiles_x, tiles_y, len(CANDIDATES), freqs, width, 2 * points), jnp.float32
            ),
            pltpu.VMEM((tiles_x, tiles_y, freqs) + slabs, jnp.bfloat16),
            pltpu.VMEM((tiles_x, freqs) + slabs, jnp.bfloat16),
            pltpu.VMEM((tiles_x, freqs) + slabs, jnp.bfloat16),
            pltpu.VMEM((tiles_y + 2, freqs) + slabs, jnp.bfloat16),
            pltpu.VMEM((2, 128, traces), jnp.bfloat16),
            pltpu.VMEM((2 * width, 2 * traces), jnp.bfloat16),
            dma((chunks,)),
            dma((nz, chunks)),
            dma((nz, tiles_x, freqs)),
            dma((nz, tiles_x, freqs)),
            dma((nz, tiles_y + 2, freqs)),
            dma((nz, chunks)),
            dma((nz, chunks)),
            dma((nz, tiles_x, freqs)),
            dma((nz, tiles_x, freqs)),
            dma((nz, tiles_y + 2, freqs)),
        ],
        compiler_params=pltpu.CompilerParams(
            collective_id=0, has_side_effects=True, vmem_limit_bytes=58 * 2**20
        ),
        cost_estimate=pl.CostEstimate(
            flops=2 * chunks * len(CANDIDATES) * width * 2 * points * 2 * traces * nz,
            bytes_accessed=12 * 2**20, transcendentals=0,
        ),
    )(green, offsets.T)


def solution(mesh):
    return jax.shard_map(
        per_device,
        mesh=mesh,
        in_specs=(P("gx", "gy", None, None, "sa", None), P()),
        out_specs=P("gx", "gy", None, None, "sa", None),
        check_vma=False,
    )
```

```python
import functools

import jax
import jax.numpy as jnp
from jax import lax
from jax.experimental import pallas as pl
from jax.experimental.pallas import tpu as pltpu
from jax.sharding import PartitionSpec as P

MESH = pl.DeviceIdType.MESH
CANDIDATES = ((0, 0), (0, 1), (1, -1), (1, 0), (1, 1))


def kernel(
    nx, ny, nz, green, offsets, out, total, beyond, stage, own, up, down, right, turned, left,
    load_sem, own_sem, up_sem, down_sem, right_sem, end_sem,
    send_zu, send_zd, send_yu, send_yd, send_x, send_end,
):
    freqs, _, halves, tiles_x, tiles_y, _, traces, lanes = own.shape
    points = halves * lanes
    width = points // nz
    phases = halves * freqs
    pairs = offsets.shape[1]
    gx, gy, gz = lax.axis_index("gx"), lax.axis_index("gy"), lax.axis_index("sa")
    has_right, has_left = gx < nx - 1, gx > 0
    has_up, has_down = gy < ny - 1, gy > 0
    has_above, has_below = gz < nz - 1, gz > 0
    inside = has_above & has_below
    raw_up, raw_down = gz < nz - 2, gz > 1
    near_top, near_bottom = gz == nz - 2, gz == 1
    near = near_top | near_bottom
    beside_end = jnp.where(near_top, gz + 1, gz - 1)

    def remote(src, dst, send, recv, **where):
        return pltpu.make_async_remote_copy(
            src_ref=src, dst_ref=dst, send_sem=send, recv_sem=recv, device_id=where, device_id_type=MESH
        )

    def load(f, h):
        columns = pl.ds(pl.multiple_of(h * lanes, lanes), lanes)
        return pltpu.make_async_copy(
            green.at[:, :, f, :, :, columns], own.at[f, gz, h], load_sem.at[f, h]
        )

    def z_up(f, slab, h):
        here = own.at[f, slab, h]
        return remote(here, here, send_zu.at[f, slab, h], own_sem.at[f, slab, h], sa=gz + 1)

    def z_down(f, slab, h):
        here = own.at[f, slab, h]
        return remote(here, here, send_zd.at[f, slab, h], own_sem.at[f, slab, h], sa=gz - 1)

    def y_down(f, slab, h):
        return remote(
            own.at[f, slab, h, :, 0], up.at[f, slab, h],
            send_yd.at[f, slab, h], up_sem.at[f, slab, h], gy=gy - 1,
        )

    def y_up(f, slab, h):
        return remote(
            own.at[f, slab, h, :, tiles_y - 1], down.at[f, slab, h],
            send_yu.at[f, slab, h], down_sem.at[f, slab, h], gy=gy + 1,
        )

    def x_left(kind, f, slab, h):
        src, dst = (
            (own.at[f, slab, h, 0], right.at[f, slab, h, pl.ds(1, tiles_y)]),
            (up.at[f, slab, h, 0], right.at[f, slab, h, tiles_y + 1]),
            (down.at[f, slab, h, 0], right.at[f, slab, h, 0]),
        )[kind]
        return remote(
            src, dst, send_x.at[kind, f, slab, h], right_sem.at[kind, f, slab, h], gx=gx - 1
        )

    def to_end(f, h, part):
        columns = pl.ds(pl.multiple_of(part * points + h * lanes, lanes), lanes)
        return remote(
            stage.at[:, :, :, f, :, columns], out.at[:, :, :, f, :, columns],
            send_end.at[f, h, part], end_sem.at[f, h, part], sa=beside_end,
        )

    def each(count, body, start=0):
        def step(i, carry):
            body(i)
            return carry

        lax.fori_loop(start, count, step, 0)

    def each_half(body):
        each(phases, lambda u: body(u // halves, u % halves))

    each_half(lambda f, h: load(f, h).start())

    barrier = pltpu.get_barrier_semaphore()
    sides = (
        (has_above, dict(sa=gz + 1)), (has_below, dict(sa=gz - 1)),
        (has_up, dict(gy=gy + 1)), (has_down, dict(gy=gy - 1)),
        (has_right, dict(gx=gx + 1)), (has_left, dict(gx=gx - 1)),
    )
    for there, where in sides:
        @pl.when(there)
        def _():
            pl.semaphore_signal(barrier, inc=1, device_id=where, device_id_type=MESH)
    pl.semaphore_wait(barrier, sum(there.astype(jnp.int32) for there, _ in sides))

    def push(f, slab, h):
        pl.when(has_down)(lambda: y_down(f, slab, h).start())
        pl.when(has_up)(lambda: y_up(f, slab, h).start())
        pl.when(has_left)(lambda: x_left(0, f, slab, h).start())

    def halo(f, slab, h):
        @pl.when(has_up)
        def _():
            y_down(f, slab, h).wait_recv()
            pl.when(has_left)(lambda: x_left(1, f, slab, h).start())

        @pl.when(has_down)
        def _():
            y_up(f, slab, h).wait_recv()
            pl.when(has_left)(lambda: x_left(2, f, slab, h).start())

        @pl.when(has_right)
        def _():
            x_left(0, f, slab, h).wait_recv()
            pl.when(has_up)(lambda: x_left(1, f, slab, h).wait_recv())
            pl.when(has_down)(lambda: x_left(2, f, slab, h).wait_recv())

    def send_own(u):
        f, v = u // halves, u % halves
        pl.when(raw_up)(lambda: z_up(f, gz, 1 - v).start())
        pl.when(raw_down)(lambda: z_down(f, gz, v).start())

    mine = gz * width // lanes
    row_at = pl.multiple_of(gz * width % lanes, width)
    row_beyond = pl.multiple_of(beside_end * width % lanes, width)

    def products(f, slab, h, both):
        rows = 4 * width if both else 2 * width
        for tx in range(tiles_x):
            for ty in range(tiles_y):
                for part in range(2):
                    turned[part] = own[f, slab, mine, tx, ty, part].T
                for base, start in ((0, row_at), (2 * width, row_beyond))[: 2 if both else 1]:
                    real = turned[0, pl.ds(start, width), :]
                    imag = turned[1, pl.ds(start, width), :]
                    left[base : base + width, :traces] = real
                    left[base : base + width, traces:] = imag
                    left[base + width : base + 2 * width, :traces] = -imag
                    left[base + width : base + 2 * width, traces:] = real
                for c, (dx, dy) in enumerate(CANDIDATES):
                    ox, oy = tx + dx, ty + dy
                    there = True
                    if ox == tiles_x:
                        there = has_right
                        beside = right.at[f, slab, h, oy + 1]
                    elif oy == tiles_y:
                        beside = up.at[f, slab, h, ox]
                    elif oy < 0:
                        beside = down.at[f, slab, h, ox]
                    else:
                        beside = own.at[f, slab, h, ox, oy]
                    if oy == tiles_y:
                        there = there & has_up
                    if oy < 0:
                        there = there & has_down

                    def add(beside=beside, c=c):
                        block = jnp.dot(
                            left[:rows], beside[...].reshape(2 * traces, lanes),
                            preferred_element_type=jnp.float32,
                        )
                        total[f, tx, ty, c, h, :, :lanes] += block[:width]
                        total[f, tx, ty, c, h, :, lanes:] += block[width : 2 * width]
                        if both:
                            beyond[f, tx, ty, c, h, :, :lanes] += block[2 * width : 3 * width]
                            beyond[f, tx, ty, c, h, :, lanes:] += block[3 * width :]

                    if there is True:
                        add()
                    else:
                        pl.when(there)(add)

    def choose(f, h, source, target, add):
        for k in range(pairs):
            wanted = offsets[1, k] + 3 * offsets[0, k]
            for tx in range(tiles_x):
                for ty in range(tiles_y):
                    for part in range(2):
                        columns = pl.ds(pl.multiple_of(part * points + h * lanes, lanes), lanes)
                        value = source[f, tx, ty, wanted, h, :, part * lanes : (part + 1) * lanes]
                        if add:
                            value = value + target[tx, ty, k, f, :, columns]
                        target[tx, ty, k, f, :, columns] = value

    def take(f, h):
        load(f, h).wait()
        push(f, gz, h)

    each(halves, lambda h: load(0, h).wait())
    send_own(0)
    each(halves, lambda h: push(0, gz, h))
    each(phases, lambda u: take(u // halves, u % halves), halves)
    total[...] = jnp.zeros_like(total)

    @pl.when(jnp.logical_not(inside))
    def _():
        each(phases, send_own, 1)

        def own_part(f, h):
            halo(f, gz, h)
            products(f, gz, h, False)

        each_half(own_part)

        def receive(f, v):
            h = jnp.where(gz == 0, v, 1 - v)
            for part in range(2):
                to_end(f, h, part).wait_recv()
            choose(f, h, total, out, True)

        each_half(receive)

    @pl.when(inside)
    def _():
        beyond[...] = jnp.zeros_like(beyond)

        def phase(f, v):
            u = f * halves + v
            near_h = jnp.where(near_top, 1 - v, v)

            def at(d):
                lower, upper = gz - d, gz + d

                @pl.when(lower >= 0)
                def _():
                    z_up(f, lower, 1 - v).wait_recv()
                    pl.when(raw_up)(lambda: z_up(f, lower, 1 - v).start())
                    push(f, lower, 1 - v)

                @pl.when(upper < nz)
                def _():
                    z_down(f, upper, v).wait_recv()
                    pl.when(raw_down)(lambda: z_down(f, upper, v).start())
                    push(f, upper, v)

                pl.when((d == 1) & (u + 1 < phases))(lambda: send_own(u + 1))

                @pl.when((d == 1) & (v == 0) & near)
                def _():
                    def own_part(h):
                        halo(f, gz, h)
                        products(f, gz, h, True)

                    each(halves, own_part)

                slab = jnp.where(near_top, lower, upper)

                @pl.when(near & (slab >= 0) & (slab < nz))
                def _():
                    halo(f, slab, near_h)
                    products(f, slab, near_h, True)

            each(nz, at, 1)

            @pl.when(near)
            def _():
                choose(f, near_h, beyond, stage, False)
                for part in range(2):
                    to_end(f, near_h, part).start()

            @pl.when(v == halves - 1)
            def _():
                def rest(slab):
                    done = (near_top & (slab <= gz)) | (near_bottom & (slab >= gz))

                    @pl.when(jnp.logical_not(done))
                    def _():
                        def part(h):
                            halo(f, slab, h)
                            products(f, slab, h, False)

                        each(halves, part)

                each(nz, rest)
                each(halves, lambda h: choose(f, h, total, out, False))

        each_half(phase)

    def finish(slab):
        def body(f, h):
            pl.when(raw_up & (slab <= gz))(lambda: z_up(f, slab, h).wait_send())
            pl.when(raw_down & (slab >= gz))(lambda: z_down(f, slab, h).wait_send())

            @pl.when(inside | (slab == gz))
            def _():
                pl.when(has_down)(lambda: y_down(f, slab, h).wait_send())
                pl.when(has_up)(lambda: y_up(f, slab, h).wait_send())

                @pl.when(has_left)
                def _():
                    x_left(0, f, slab, h).wait_send()
                    pl.when(has_up)(lambda: x_left(1, f, slab, h).wait_send())
                    pl.when(has_down)(lambda: x_left(2, f, slab, h).wait_send())

        each_half(body)

    each(nz, finish)

    @pl.when(near)
    def _():
        def body(f, h):
            for part in range(2):
                to_end(f, h, part).wait_send()

        each_half(body)


def per_device(green, offsets):
    tiles_x, tiles_y, freqs, _, traces, points = green.shape
    nx, ny, nz = (lax.axis_size(name) for name in ("gx", "gy", "sa"))
    width, lanes, pairs = points // nz, 128, offsets.shape[0]
    halves = points // lanes
    dma = pltpu.SemaphoreType.DMA
    result = (tiles_x, tiles_y, pairs, freqs, width, 2 * points)
    sums = (freqs, tiles_x, tiles_y, len(CANDIDATES), halves, width, 2 * lanes)
    piece, cell = (freqs, nz, halves), (2, traces, lanes)
    return pl.pallas_call(
        functools.partial(kernel, nx, ny, nz),
        out_shape=jax.ShapeDtypeStruct(result, jnp.float32),
        in_specs=[pl.BlockSpec(memory_space=pl.ANY), pl.BlockSpec(memory_space=pltpu.SMEM)],
        out_specs=pl.BlockSpec(memory_space=pltpu.VMEM),
        scratch_shapes=[
            pltpu.VMEM(sums, jnp.float32),
            pltpu.VMEM(sums, jnp.float32),
            pltpu.VMEM(result, jnp.float32),
            pltpu.VMEM(piece + (tiles_x, tiles_y) + cell, jnp.bfloat16),
            pltpu.VMEM(piece + (tiles_x,) + cell, jnp.bfloat16),
            pltpu.VMEM(piece + (tiles_x,) + cell, jnp.bfloat16),
            pltpu.VMEM(piece + (tiles_y + 2,) + cell, jnp.bfloat16),
            pltpu.VMEM((2, lanes, traces), jnp.bfloat16),
            pltpu.VMEM((4 * width, 2 * traces), jnp.bfloat16),
            dma((freqs, halves)),
            dma(piece),
            dma(piece),
            dma(piece),
            dma((3,) + piece),
            dma((freqs, halves, 2)),
            dma(piece),
            dma(piece),
            dma(piece),
            dma(piece),
            dma((3,) + piece),
            dma((freqs, halves, 2)),
        ],
        compiler_params=pltpu.CompilerParams(
            collective_id=0, has_side_effects=True, vmem_limit_bytes=61 * 2**20
        ),
        cost_estimate=pl.CostEstimate(
            flops=2 * tiles_x * tiles_y * freqs * len(CANDIDATES) * width * 2 * points * 2 * traces * nz,
            bytes_accessed=12 * 2**20, transcendentals=0,
        ),
    )(green, offsets.T)


def solution(mesh):
    return jax.shard_map(
        per_device,
        mesh=mesh,
        in_specs=(P("gx", "gy", None, None, "sa", None), P()),
        out_specs=P("gx", "gy", None, None, "sa", None),
        check_vma=False,
    )
```

```python
import functools

import jax
import jax.numpy as jnp
from jax import lax
from jax.experimental import pallas as pl
from jax.experimental.pallas import tpu as pltpu
from jax.sharding import PartitionSpec as P

MESH = pl.DeviceIdType.MESH
CANDIDATES = ((0, 0), (0, 1), (1, -1), (1, 0), (1, 1))


def kernel(
    nx, ny, nz, green, offsets, out, total, beyond, stage, own, up, down, right, turned, left,
    load_sem, own_sem, up_sem, down_sem, right_sem, end_sem,
    send_zu, send_zd, send_yu, send_yd, send_x, send_end, send_halo,
):
    freqs, _, halves, tiles_x, tiles_y, _, traces, lanes = own.shape
    points = halves * lanes
    width = points // nz
    phases = halves * freqs
    pairs = offsets.shape[1]
    gx, gy, gz = lax.axis_index("gx"), lax.axis_index("gy"), lax.axis_index("sa")
    has_right, has_left = gx < nx - 1, gx > 0
    has_up, has_down = gy < ny - 1, gy > 0
    has_above, has_below = gz < nz - 1, gz > 0
    inside = has_above & has_below
    raw_up, raw_down = gz < nz - 2, gz > 1
    near_top, near_bottom = gz == nz - 2, gz == 1
    near = near_top | near_bottom
    at_end = jnp.logical_not(inside)
    middle = inside & jnp.logical_not(near)
    beside_end = jnp.where(near_top, gz + 1, gz - 1)
    inward = jnp.where(has_below, gz - 1, gz + 1)

    def remote(src, dst, send, recv, **where):
        return pltpu.make_async_remote_copy(
            src_ref=src, dst_ref=dst, send_sem=send, recv_sem=recv, device_id=where, device_id_type=MESH
        )

    def load(f, h):
        columns = pl.ds(pl.multiple_of(h * lanes, lanes), lanes)
        return pltpu.make_async_copy(
            green.at[:, :, f, :, :, columns], own.at[f, gz, h], load_sem.at[f, h]
        )

    def z_up(f, slab, h):
        here = own.at[f, slab, h]
        return remote(here, here, send_zu.at[f, slab, h], own_sem.at[f, slab, h], sa=gz + 1)

    def z_down(f, slab, h):
        here = own.at[f, slab, h]
        return remote(here, here, send_zd.at[f, slab, h], own_sem.at[f, slab, h], sa=gz - 1)

    def y_down(f, slab, h):
        return remote(
            own.at[f, slab, h, :, 0], up.at[f, slab, h],
            send_yd.at[f, slab, h], up_sem.at[f, slab, h], gy=gy - 1,
        )

    def y_up(f, slab, h):
        return remote(
            own.at[f, slab, h, :, tiles_y - 1], down.at[f, slab, h],
            send_yu.at[f, slab, h], down_sem.at[f, slab, h], gy=gy + 1,
        )

    def x_left(kind, f, slab, h):
        src, dst = (
            (own.at[f, slab, h, 0], right.at[f, slab, h, pl.ds(1, tiles_y)]),
            (up.at[f, slab, h, 0], right.at[f, slab, h, tiles_y + 1]),
            (down.at[f, slab, h, 0], right.at[f, slab, h, 0]),
        )[kind]
        return remote(
            src, dst, send_x.at[kind, f, slab, h], right_sem.at[kind, f, slab, h], gx=gx - 1
        )

    def to_end(f, h, part):
        columns = pl.ds(pl.multiple_of(part * points + h * lanes, lanes), lanes)
        return remote(
            stage.at[:, :, :, f, :, columns], out.at[:, :, :, f, :, columns],
            send_end.at[f, h, part], end_sem.at[f, h, part], sa=beside_end,
        )

    def halo_up(f, h):
        here = up.at[f, gz, h]
        return remote(here, here, send_halo.at[0, f, h], up_sem.at[f, gz, h], sa=inward)

    def halo_down(f, h):
        here = down.at[f, gz, h]
        return remote(here, here, send_halo.at[1, f, h], down_sem.at[f, gz, h], sa=inward)

    def each(count, body, start=0):
        def step(i, carry):
            body(i)
            return carry

        lax.fori_loop(start, count, step, 0)

    def each_half(body):
        each(phases, lambda u: body(u // halves, u % halves))

    each_half(lambda f, h: load(f, h).start())

    barrier = pltpu.get_barrier_semaphore()
    sides = (
        (has_above, dict(sa=gz + 1)), (has_below, dict(sa=gz - 1)),
        (has_up, dict(gy=gy + 1)), (has_down, dict(gy=gy - 1)),
        (has_right, dict(gx=gx + 1)), (has_left, dict(gx=gx - 1)),
    )
    for there, where in sides:
        @pl.when(there)
        def _():
            pl.semaphore_signal(barrier, inc=1, device_id=where, device_id_type=MESH)
    pl.semaphore_wait(barrier, sum(there.astype(jnp.int32) for there, _ in sides))

    def push_x(f, slab, h):
        pl.when(has_left)(lambda: x_left(0, f, slab, h).start())

    def push(f, slab, h):
        pl.when(has_down)(lambda: y_down(f, slab, h).start())
        pl.when(has_up)(lambda: y_up(f, slab, h).start())
        push_x(f, slab, h)

    def halo_y(f, slab, h):
        @pl.when(has_up)
        def _():
            y_down(f, slab, h).wait_recv()
            pl.when(has_left)(lambda: x_left(1, f, slab, h).start())

        @pl.when(has_down)
        def _():
            y_up(f, slab, h).wait_recv()
            pl.when(has_left)(lambda: x_left(2, f, slab, h).start())

    def halo_x(f, slab, h):
        @pl.when(has_right)
        def _():
            x_left(0, f, slab, h).wait_recv()
            pl.when(has_up)(lambda: x_left(1, f, slab, h).wait_recv())
            pl.when(has_down)(lambda: x_left(2, f, slab, h).wait_recv())

    def send_own(u):
        f, v = u // halves, u % halves
        pl.when(raw_up)(lambda: z_up(f, gz, 1 - v).start())
        pl.when(raw_down)(lambda: z_down(f, gz, v).start())

    mine = gz * width // lanes
    row_at = pl.multiple_of(gz * width % lanes, width)
    row_beyond = pl.multiple_of(beside_end * width % lanes, width)

    def products(f, slab, h, both):
        rows = 4 * width if both else 2 * width
        for tx in range(tiles_x):
            for ty in range(tiles_y):
                for part in range(2):
                    turned[part] = own[f, slab, mine, tx, ty, part].T
                for base, start in ((0, row_at), (2 * width, row_beyond))[: 2 if both else 1]:
                    real = turned[0, pl.ds(start, width), :]
                    imag = turned[1, pl.ds(start, width), :]
                    left[base : base + width, :traces] = real
                    left[base : base + width, traces:] = imag
                    left[base + width : base + 2 * width, :traces] = -imag
                    left[base + width : base + 2 * width, traces:] = real
                for c, (dx, dy) in enumerate(CANDIDATES):
                    ox, oy = tx + dx, ty + dy
                    there = True
                    if ox == tiles_x:
                        there = has_right
                        beside = right.at[f, slab, h, oy + 1]
                    elif oy == tiles_y:
                        beside = up.at[f, slab, h, ox]
                    elif oy < 0:
                        beside = down.at[f, slab, h, ox]
                    else:
                        beside = own.at[f, slab, h, ox, oy]
                    if oy == tiles_y:
                        there = there & has_up
                    if oy < 0:
                        there = there & has_down

                    def add(beside=beside, c=c):
                        block = jnp.dot(
                            left[:rows], beside[...].reshape(2 * traces, lanes),
                            preferred_element_type=jnp.float32,
                        )
                        total[f, tx, ty, c, h, :, :lanes] += block[:width]
                        total[f, tx, ty, c, h, :, lanes:] += block[width : 2 * width]
                        if both:
                            beyond[f, tx, ty, c, h, :, :lanes] += block[2 * width : 3 * width]
                            beyond[f, tx, ty, c, h, :, lanes:] += block[3 * width :]

                    if there is True:
                        add()
                    else:
                        pl.when(there)(add)

    def choose(f, h, source, target, add):
        for k in range(pairs):
            wanted = offsets[1, k] + 3 * offsets[0, k]
            for tx in range(tiles_x):
                for ty in range(tiles_y):
                    for part in range(2):
                        columns = pl.ds(pl.multiple_of(part * points + h * lanes, lanes), lanes)
                        value = source[f, tx, ty, wanted, h, :, part * lanes : (part + 1) * lanes]
                        if add:
                            value = value + target[tx, ty, k, f, :, columns]
                        target[tx, ty, k, f, :, columns] = value

    def rest(f, slab):
        each(halves, lambda h: halo_y(f, slab, h))

        def part(h):
            halo_x(f, slab, h)
            products(f, slab, h, False)

        each(halves, part)

    each(halves, lambda h: load(0, h).wait())
    send_own(0)

    @pl.when(near)
    def _():
        push(0, gz, jnp.where(near_top, 1, 0))

    each(phases, lambda u: load(u // halves, u % halves).wait(), halves)

    @pl.when(at_end)
    def _():
        each(phases, send_own, 1)
        each_half(lambda f, v: push(f, gz, jnp.where(gz == 0, v, 1 - v)))
        total[...] = jnp.zeros_like(total)

        def pass_halo(f, v):
            h = jnp.where(gz == 0, v, 1 - v)
            halo_y(f, gz, h)
            pl.when(has_up)(lambda: halo_up(f, h).start())
            pl.when(has_down)(lambda: halo_down(f, h).start())

        each_half(pass_halo)

        def own_part(f, h):
            halo_x(f, gz, h)
            products(f, gz, h, False)

        each_half(own_part)

        def receive(f, v):
            h = jnp.where(gz == 0, v, 1 - v)
            for part in range(2):
                to_end(f, h, part).wait_recv()
            choose(f, h, total, out, True)

        each_half(receive)

    @pl.when(near)
    def _():
        end = beside_end

        def pass_end(u):
            f, v = u // halves, u % halves

            @pl.when(near_top)
            def _():
                z_down(f, end, v).wait_recv()
                z_down(f, end, v).start()
                push_x(f, end, v)

            @pl.when(near_bottom)
            def _():
                z_up(f, end, 1 - v).wait_recv()
                z_up(f, end, 1 - v).start()
                push_x(f, end, 1 - v)

            pl.when(u + 1 < phases)(lambda: send_own(u + 1))

        total[...] = jnp.zeros_like(total)
        beyond[...] = jnp.zeros_like(beyond)
        pass_end(0)

        def phase(f, v):
            u = f * halves + v
            h = jnp.where(near_top, 1 - v, v)

            def at(d):
                slab = jnp.where(near_top, gz - d, gz + d)

                @pl.when(near_top)
                def _():
                    z_up(f, slab, h).wait_recv()

                @pl.when(near_bottom)
                def _():
                    z_down(f, slab, h).wait_recv()

                push(f, slab, h)
                pl.when((d == 2) & (u + 1 < phases))(lambda: pass_end(u + 1))

                @pl.when(d == 1)
                def _():
                    halo_y(f, gz, h)

                halo_y(f, slab, h)

                def work(slab):
                    halo_x(f, slab, h)
                    products(f, slab, h, True)

                @pl.when((d == 1) & (v == halves - 1) & (f > 0))
                def _():
                    rest(f - 1, end)
                    each(halves, lambda i: choose(f - 1, i, total, out, False))

                each(jnp.where(d == 1, 2, 1), lambda i: work(jnp.where((d == 1) & (i == 0), gz, slab)))

                @pl.when((d == 1) & (u + 1 < phases))
                def _():
                    later = (u + 1) % halves
                    push((u + 1) // halves, gz, jnp.where(near_top, 1 - later, later))

            each(nz - 1, at, 1)
            choose(f, h, beyond, stage, False)
            for part in range(2):
                to_end(f, h, part).start()

        each_half(phase)
        rest(freqs - 1, end)
        each(halves, lambda h: choose(freqs - 1, h, total, out, False))

    if nz > 4:
        @pl.when(middle)
        def _():
            each_half(lambda f, h: push(f, gz, h))
            total[...] = jnp.zeros_like(total)

            def phase(f, v):
                u = f * halves + v

                def at(d):
                    lower, upper = gz - d, gz + d

                    @pl.when(lower >= 0)
                    def _():
                        z_up(f, lower, 1 - v).wait_recv()
                        z_up(f, lower, 1 - v).start()
                        push(f, lower, 1 - v)

                    @pl.when(upper < nz)
                    def _():
                        z_down(f, upper, v).wait_recv()
                        z_down(f, upper, v).start()
                        push(f, upper, v)

                    pl.when((d == 1) & (u + 1 < phases))(lambda: send_own(u + 1))

                each(nz, at, 1)

                @pl.when(v == halves - 1)
                def _():
                    each(nz, lambda slab: rest(f, slab))
                    each(halves, lambda h: choose(f, h, total, out, False))

            each_half(phase)

    def finish(slab):
        def body(f, h):
            pl.when(raw_up & (slab <= gz))(lambda: z_up(f, slab, h).wait_send())
            pl.when(raw_down & (slab >= gz))(lambda: z_down(f, slab, h).wait_send())

            @pl.when(middle | (slab == gz) | (near & (slab != beside_end)))
            def _():
                pl.when(has_down)(lambda: y_down(f, slab, h).wait_send())
                pl.when(has_up)(lambda: y_up(f, slab, h).wait_send())

            @pl.when(at_end & (slab == gz))
            def _():
                pl.when(has_up)(lambda: halo_up(f, h).wait_send())
                pl.when(has_down)(lambda: halo_down(f, h).wait_send())

            @pl.when(inside | (slab == gz))
            def _():

                @pl.when(has_left)
                def _():
                    x_left(0, f, slab, h).wait_send()
                    pl.when(has_up)(lambda: x_left(1, f, slab, h).wait_send())
                    pl.when(has_down)(lambda: x_left(2, f, slab, h).wait_send())

        each_half(body)

    each(nz, finish)

    @pl.when(near)
    def _():
        def body(f, h):
            for part in range(2):
                to_end(f, h, part).wait_send()

        each_half(body)


def per_device(green, offsets):
    tiles_x, tiles_y, freqs, _, traces, points = green.shape
    nx, ny, nz = (lax.axis_size(name) for name in ("gx", "gy", "sa"))
    width, lanes, pairs = points // nz, 128, offsets.shape[0]
    halves = points // lanes
    dma = pltpu.SemaphoreType.DMA
    result = (tiles_x, tiles_y, pairs, freqs, width, 2 * points)
    sums = (freqs, tiles_x, tiles_y, len(CANDIDATES), halves, width, 2 * lanes)
    piece, cell = (freqs, nz, halves), (2, traces, lanes)
    return pl.pallas_call(
        functools.partial(kernel, nx, ny, nz),
        out_shape=jax.ShapeDtypeStruct(result, jnp.float32),
        in_specs=[pl.BlockSpec(memory_space=pl.ANY), pl.BlockSpec(memory_space=pltpu.SMEM)],
        out_specs=pl.BlockSpec(memory_space=pltpu.VMEM),
        scratch_shapes=[
            pltpu.VMEM(sums, jnp.float32),
            pltpu.VMEM(sums, jnp.float32),
            pltpu.VMEM(result, jnp.float32),
            pltpu.VMEM(piece + (tiles_x, tiles_y) + cell, jnp.bfloat16),
            pltpu.VMEM(piece + (tiles_x,) + cell, jnp.bfloat16),
            pltpu.VMEM(piece + (tiles_x,) + cell, jnp.bfloat16),
            pltpu.VMEM(piece + (tiles_y + 2,) + cell, jnp.bfloat16),
            pltpu.VMEM((2, lanes, traces), jnp.bfloat16),
            pltpu.VMEM((4 * width, 2 * traces), jnp.bfloat16),
            dma((freqs, halves)),
            dma(piece),
            dma(piece),
            dma(piece),
            dma((3,) + piece),
            dma((freqs, halves, 2)),
            dma(piece),
            dma(piece),
            dma(piece),
            dma(piece),
            dma((3,) + piece),
            dma((freqs, halves, 2)),
            dma((2, freqs, halves)),
        ],
        compiler_params=pltpu.CompilerParams(
            collective_id=0, has_side_effects=True, vmem_limit_bytes=61 * 2**20
        ),
        cost_estimate=pl.CostEstimate(
            flops=2 * tiles_x * tiles_y * freqs * len(CANDIDATES) * width * 2 * points * 2 * traces * nz,
            bytes_accessed=12 * 2**20, transcendentals=0,
        ),
    )(green, offsets.T)


def solution(mesh):
    return jax.shard_map(
        per_device,
        mesh=mesh,
        in_specs=(P("gx", "gy", None, None, "sa", None), P()),
        out_specs=P("gx", "gy", None, None, "sa", None),
        check_vma=False,
    )
```

```python
import functools

import jax
import jax.numpy as jnp
from jax import lax
from jax.experimental import pallas as pl
from jax.experimental.pallas import tpu as pltpu
from jax.sharding import PartitionSpec as P

MESH = pl.DeviceIdType.MESH
CANDIDATES = ((0, 0), (0, 1), (1, -1), (1, 0), (1, 1))


def kernel(
    nx, ny, nz, green, offsets, out, total, beyond, stage, own, up, down, right, turned, left,
    load_sem, own_sem, up_sem, down_sem, right_sem, end_sem,
    send_zu, send_zd, send_yu, send_yd, send_x, send_end, send_halo,
):
    freqs, _, halves, tiles_x, tiles_y, _, traces, lanes = own.shape
    points = halves * lanes
    width = points // nz
    phases = halves * freqs
    pairs = offsets.shape[1]
    gx, gy, gz = lax.axis_index("gx"), lax.axis_index("gy"), lax.axis_index("sa")
    has_right, has_left = gx < nx - 1, gx > 0
    has_up, has_down = gy < ny - 1, gy > 0
    has_above, has_below = gz < nz - 1, gz > 0
    inside = has_above & has_below
    raw_up, raw_down = gz < nz - 2, gz > 1
    near_top, near_bottom = gz == nz - 2, gz == 1
    near = near_top | near_bottom
    at_end = jnp.logical_not(inside)
    middle = inside & jnp.logical_not(near)
    beside_end = jnp.where(near_top, gz + 1, gz - 1)
    inward = jnp.where(has_below, gz - 1, gz + 1)

    def remote(src, dst, send, recv, **where):
        return pltpu.make_async_remote_copy(
            src_ref=src, dst_ref=dst, send_sem=send, recv_sem=recv, device_id=where, device_id_type=MESH
        )

    def load(f, h):
        columns = pl.ds(pl.multiple_of(h * lanes, lanes), lanes)
        return pltpu.make_async_copy(
            green.at[:, :, f, :, :, columns], own.at[f, gz, h], load_sem.at[f, h]
        )

    def z_up(f, slab, h):
        here = own.at[f, slab, h]
        return remote(here, here, send_zu.at[f, slab, h], own_sem.at[f, slab, h], sa=gz + 1)

    def z_down(f, slab, h):
        here = own.at[f, slab, h]
        return remote(here, here, send_zd.at[f, slab, h], own_sem.at[f, slab, h], sa=gz - 1)

    def y_down(f, slab, h):
        return remote(
            own.at[f, slab, h, :, 0], up.at[f, slab, h],
            send_yd.at[f, slab, h], up_sem.at[f, slab, h], gy=gy - 1,
        )

    def y_up(f, slab, h):
        return remote(
            own.at[f, slab, h, :, tiles_y - 1], down.at[f, slab, h],
            send_yu.at[f, slab, h], down_sem.at[f, slab, h], gy=gy + 1,
        )

    def x_left(kind, f, slab, h):
        src, dst = (
            (own.at[f, slab, h, 0], right.at[f, slab, h, pl.ds(1, tiles_y)]),
            (up.at[f, slab, h, 0], right.at[f, slab, h, tiles_y + 1]),
            (down.at[f, slab, h, 0], right.at[f, slab, h, 0]),
        )[kind]
        return remote(
            src, dst, send_x.at[kind, f, slab, h], right_sem.at[kind, f, slab, h], gx=gx - 1
        )

    def to_end(f, h, part):
        columns = pl.ds(pl.multiple_of(part * points + h * lanes, lanes), lanes)
        return remote(
            stage.at[:, :, :, f, :, columns], out.at[:, :, :, f, :, columns],
            send_end.at[f, h, part], end_sem.at[f, h, part], sa=beside_end,
        )

    def halo_up(f, h):
        here = up.at[f, gz, h]
        return remote(here, here, send_halo.at[0, f, h], up_sem.at[f, gz, h], sa=inward)

    def halo_down(f, h):
        here = down.at[f, gz, h]
        return remote(here, here, send_halo.at[1, f, h], down_sem.at[f, gz, h], sa=inward)

    def each(count, body, start=0):
        def step(i, carry):
            body(i)
            return carry

        lax.fori_loop(start, count, step, 0)

    def each_half(body):
        each(phases, lambda u: body(u // halves, u % halves))

    each_half(lambda f, h: load(f, h).start())

    barrier = pltpu.get_barrier_semaphore()
    sides = (
        (has_above, dict(sa=gz + 1)), (has_below, dict(sa=gz - 1)),
        (has_up, dict(gy=gy + 1)), (has_down, dict(gy=gy - 1)),
        (has_right, dict(gx=gx + 1)), (has_left, dict(gx=gx - 1)),
    )
    for there, where in sides:
        @pl.when(there)
        def _():
            pl.semaphore_signal(barrier, inc=1, device_id=where, device_id_type=MESH)
    pl.semaphore_wait(barrier, sum(there.astype(jnp.int32) for there, _ in sides))

    def push_x(f, slab, h):
        pl.when(has_left)(lambda: x_left(0, f, slab, h).start())

    def push(f, slab, h):
        pl.when(has_down)(lambda: y_down(f, slab, h).start())
        pl.when(has_up)(lambda: y_up(f, slab, h).start())
        push_x(f, slab, h)

    def halo_y(f, slab, h):
        @pl.when(has_up)
        def _():
            y_down(f, slab, h).wait_recv()
            pl.when(has_left)(lambda: x_left(1, f, slab, h).start())

        @pl.when(has_down)
        def _():
            y_up(f, slab, h).wait_recv()
            pl.when(has_left)(lambda: x_left(2, f, slab, h).start())

    def halo_x(f, slab, h):
        @pl.when(has_right)
        def _():
            x_left(0, f, slab, h).wait_recv()
            pl.when(has_up)(lambda: x_left(1, f, slab, h).wait_recv())
            pl.when(has_down)(lambda: x_left(2, f, slab, h).wait_recv())

    def send_own(u):
        f, v = u // halves, u % halves
        pl.when(raw_up)(lambda: z_up(f, gz, 1 - v).start())
        pl.when(raw_down)(lambda: z_down(f, gz, v).start())

    mine = gz * width // lanes
    row_at = pl.multiple_of(gz * width % lanes, width)
    row_beyond = pl.multiple_of(beside_end * width % lanes, width)

    def products(f, slab, h, both):
        rows = 4 * width if both else 2 * width
        for tx in range(tiles_x):
            for ty in range(tiles_y):
                for part in range(2):
                    turned[part] = own[f, slab, mine, tx, ty, part].T
                for base, start in ((0, row_at), (2 * width, row_beyond))[: 2 if both else 1]:
                    real = turned[0, pl.ds(start, width), :]
                    imag = turned[1, pl.ds(start, width), :]
                    left[base : base + width, :traces] = real
                    left[base : base + width, traces:] = imag
                    left[base + width : base + 2 * width, :traces] = -imag
                    left[base + width : base + 2 * width, traces:] = real
                for c, (dx, dy) in enumerate(CANDIDATES):
                    ox, oy = tx + dx, ty + dy
                    there = True
                    if ox == tiles_x:
                        there = has_right
                        beside = right.at[f, slab, h, oy + 1]
                    elif oy == tiles_y:
                        beside = up.at[f, slab, h, ox]
                    elif oy < 0:
                        beside = down.at[f, slab, h, ox]
                    else:
                        beside = own.at[f, slab, h, ox, oy]
                    if oy == tiles_y:
                        there = there & has_up
                    if oy < 0:
                        there = there & has_down

                    def add(beside=beside, c=c):
                        block = jnp.dot(
                            left[:rows], beside[...].reshape(2 * traces, lanes),
                            preferred_element_type=jnp.float32,
                        )
                        total[f, tx, ty, c, h, :, :lanes] += block[:width]
                        total[f, tx, ty, c, h, :, lanes:] += block[width : 2 * width]
                        if both:
                            beyond[f, tx, ty, c, h, :, :lanes] += block[2 * width : 3 * width]
                            beyond[f, tx, ty, c, h, :, lanes:] += block[3 * width :]

                    if there is True:
                        add()
                    else:
                        pl.when(there)(add)

    def choose(f, h, source, target, add):
        for k in range(pairs):
            wanted = offsets[1, k] + 3 * offsets[0, k]
            for tx in range(tiles_x):
                for ty in range(tiles_y):
                    for part in range(2):
                        columns = pl.ds(pl.multiple_of(part * points + h * lanes, lanes), lanes)
                        value = source[f, tx, ty, wanted, h, :, part * lanes : (part + 1) * lanes]
                        if add:
                            value = value + target[tx, ty, k, f, :, columns]
                        target[tx, ty, k, f, :, columns] = value

    def rest(f, slab):
        each(halves, lambda h: halo_y(f, slab, h))

        def part(h):
            halo_x(f, slab, h)
            products(f, slab, h, False)

        each(halves, part)

    each(halves, lambda h: load(0, h).wait())
    send_own(0)

    @pl.when(near)
    def _():
        push(0, gz, jnp.where(near_top, 1, 0))

    each(phases, lambda u: load(u // halves, u % halves).wait(), halves)

    @pl.when(at_end)
    def _():
        each(phases, send_own, 1)
        each_half(lambda f, v: push(f, gz, jnp.where(gz == 0, v, 1 - v)))
        total[...] = jnp.zeros_like(total)

        def pass_halo(f, v):
            h = jnp.where(gz == 0, v, 1 - v)
            halo_y(f, gz, h)
            pl.when(has_up)(lambda: halo_up(f, h).start())
            pl.when(has_down)(lambda: halo_down(f, h).start())

        each_half(pass_halo)

        def own_part(f, h):
            halo_x(f, gz, h)
            products(f, gz, h, False)

        each_half(own_part)

        def receive(f, v):
            h = jnp.where(gz == 0, v, 1 - v)
            for part in range(2):
                to_end(f, h, part).wait_recv()
            choose(f, h, total, out, True)

        each_half(receive)

    @pl.when(near)
    def _():
        end = beside_end

        def pass_end(u):
            f, v = u // halves, u % halves

            @pl.when(near_top)
            def _():
                z_down(f, end, v).wait_recv()
                z_down(f, end, v).start()
                push_x(f, end, v)

            @pl.when(near_bottom)
            def _():
                z_up(f, end, 1 - v).wait_recv()
                z_up(f, end, 1 - v).start()
                push_x(f, end, 1 - v)

            pl.when(u + 1 < phases)(lambda: send_own(u + 1))

        total[...] = jnp.zeros_like(total)
        beyond[...] = jnp.zeros_like(beyond)

        def near_half(v):
            return jnp.where(near_top, 1 - v, v)

        def work(f, slab, h):
            halo_y(f, slab, h)
            halo_x(f, slab, h)
            products(f, slab, h, True)

        work(0, gz, near_half(0))
        pass_end(0)

        def rest_half(f, v):
            h = jnp.where(near_top, v, 1 - v)
            halo_y(f, end, h)
            halo_x(f, end, h)
            products(f, end, h, False)

        def phase(f, v):
            u = f * halves + v
            more = u + 1 < phases
            h = near_half(v)
            next_f, next_h = (u + 1) // halves, near_half((u + 1) % halves)

            def at(d):
                slab = jnp.where(near_top, gz - d, gz + d)

                @pl.when(near_top)
                def _():
                    z_up(f, slab, h).wait_recv()

                @pl.when(near_bottom)
                def _():
                    z_down(f, slab, h).wait_recv()

                push(f, slab, h)
                pl.when((d == 1) & more)(lambda: push(next_f, gz, next_h))
                pl.when((d == 2) & more)(lambda: pass_end(u + 1))
                pl.when((d == 1) & (f > 0))(lambda: rest_half(f - 1, v))
                first = jnp.where((d == 2) & more, 0, 1)

                def one(i):
                    own_turn = i == 0
                    work(
                        jnp.where(own_turn, next_f, f),
                        jnp.where(own_turn, gz, slab),
                        jnp.where(own_turn, next_h, h),
                    )

                each(2, one, first)

            each(nz - 1, at, 1)
            choose(f, h, beyond, stage, False)
            for part in range(2):
                to_end(f, h, part).start()

            @pl.when((v == halves - 1) & (f > 0))
            def _():
                each(halves, lambda i: choose(f - 1, i, total, out, False))

        each_half(phase)
        each(halves, lambda v: rest_half(freqs - 1, v))
        each(halves, lambda h: choose(freqs - 1, h, total, out, False))

    if nz > 4:
        @pl.when(middle)
        def _():
            each_half(lambda f, h: push(f, gz, h))
            total[...] = jnp.zeros_like(total)

            def phase(f, v):
                u = f * halves + v

                def at(d):
                    lower, upper = gz - d, gz + d

                    @pl.when(lower >= 0)
                    def _():
                        z_up(f, lower, 1 - v).wait_recv()
                        z_up(f, lower, 1 - v).start()
                        push(f, lower, 1 - v)

                    @pl.when(upper < nz)
                    def _():
                        z_down(f, upper, v).wait_recv()
                        z_down(f, upper, v).start()
                        push(f, upper, v)

                    pl.when((d == 1) & (u + 1 < phases))(lambda: send_own(u + 1))

                each(nz, at, 1)

                @pl.when(v == halves - 1)
                def _():
                    each(nz, lambda slab: rest(f, slab))
                    each(halves, lambda h: choose(f, h, total, out, False))

            each_half(phase)

    def finish(slab):
        def body(f, h):
            pl.when(raw_up & (slab <= gz))(lambda: z_up(f, slab, h).wait_send())
            pl.when(raw_down & (slab >= gz))(lambda: z_down(f, slab, h).wait_send())

            @pl.when(middle | (slab == gz) | (near & (slab != beside_end)))
            def _():
                pl.when(has_down)(lambda: y_down(f, slab, h).wait_send())
                pl.when(has_up)(lambda: y_up(f, slab, h).wait_send())

            @pl.when(at_end & (slab == gz))
            def _():
                pl.when(has_up)(lambda: halo_up(f, h).wait_send())
                pl.when(has_down)(lambda: halo_down(f, h).wait_send())

            @pl.when(inside | (slab == gz))
            def _():

                @pl.when(has_left)
                def _():
                    x_left(0, f, slab, h).wait_send()
                    pl.when(has_up)(lambda: x_left(1, f, slab, h).wait_send())
                    pl.when(has_down)(lambda: x_left(2, f, slab, h).wait_send())

        each_half(body)

    each(nz, finish)

    @pl.when(near)
    def _():
        def body(f, h):
            for part in range(2):
                to_end(f, h, part).wait_send()

        each_half(body)


def per_device(green, offsets):
    tiles_x, tiles_y, freqs, _, traces, points = green.shape
    nx, ny, nz = (lax.axis_size(name) for name in ("gx", "gy", "sa"))
    width, lanes, pairs = points // nz, 128, offsets.shape[0]
    halves = points // lanes
    dma = pltpu.SemaphoreType.DMA
    result = (tiles_x, tiles_y, pairs, freqs, width, 2 * points)
    sums = (freqs, tiles_x, tiles_y, len(CANDIDATES), halves, width, 2 * lanes)
    piece, cell = (freqs, nz, halves), (2, traces, lanes)
    return pl.pallas_call(
        functools.partial(kernel, nx, ny, nz),
        out_shape=jax.ShapeDtypeStruct(result, jnp.float32),
        in_specs=[pl.BlockSpec(memory_space=pl.ANY), pl.BlockSpec(memory_space=pltpu.SMEM)],
        out_specs=pl.BlockSpec(memory_space=pltpu.VMEM),
        scratch_shapes=[
            pltpu.VMEM(sums, jnp.float32),
            pltpu.VMEM(sums, jnp.float32),
            pltpu.VMEM(result, jnp.float32),
            pltpu.VMEM(piece + (tiles_x, tiles_y) + cell, jnp.bfloat16),
            pltpu.VMEM(piece + (tiles_x,) + cell, jnp.bfloat16),
            pltpu.VMEM(piece + (tiles_x,) + cell, jnp.bfloat16),
            pltpu.VMEM(piece + (tiles_y + 2,) + cell, jnp.bfloat16),
            pltpu.VMEM((2, lanes, traces), jnp.bfloat16),
            pltpu.VMEM((4 * width, 2 * traces), jnp.bfloat16),
            dma((freqs, halves)),
            dma(piece),
            dma(piece),
            dma(piece),
            dma((3,) + piece),
            dma((freqs, halves, 2)),
            dma(piece),
            dma(piece),
            dma(piece),
            dma(piece),
            dma((3,) + piece),
            dma((freqs, halves, 2)),
            dma((2, freqs, halves)),
        ],
        compiler_params=pltpu.CompilerParams(
            collective_id=0, has_side_effects=True, vmem_limit_bytes=61 * 2**20
        ),
        cost_estimate=pl.CostEstimate(
            flops=2 * tiles_x * tiles_y * freqs * len(CANDIDATES) * width * 2 * points * 2 * traces * nz,
            bytes_accessed=12 * 2**20, transcendentals=0,
        ),
    )(green, offsets.T)


def solution(mesh):
    return jax.shard_map(
        per_device,
        mesh=mesh,
        in_specs=(P("gx", "gy", None, None, "sa", None), P()),
        out_specs=P("gx", "gy", None, None, "sa", None),
        check_vma=False,
    )
```

```python
import functools

import jax
import jax.numpy as jnp
from jax import lax
from jax.experimental import pallas as pl
from jax.experimental.pallas import tpu as pltpu
from jax.sharding import PartitionSpec as P

MESH = pl.DeviceIdType.MESH
CANDIDATES = ((0, 0), (0, 1), (1, -1), (1, 0), (1, 1))
GROUPS = ((0, 3), (1, 4), (2,))


def kernel(
    nx, ny, nz, green, offsets, out, total, beyond, stage, own, up, down, right, turned, left,
    load_sem, own_sem, up_sem, down_sem, right_sem, end_sem,
    send_zu, send_zd, send_yu, send_yd, send_x, send_end, send_halo,
):
    freqs, _, halves, tiles_x, tiles_y, _, traces, lanes = own.shape
    points = halves * lanes
    width = points // nz
    phases = halves * freqs
    pairs = offsets.shape[1]
    gx, gy, gz = lax.axis_index("gx"), lax.axis_index("gy"), lax.axis_index("sa")
    has_right, has_left = gx < nx - 1, gx > 0
    has_up, has_down = gy < ny - 1, gy > 0
    has_above, has_below = gz < nz - 1, gz > 0
    inside = has_above & has_below
    raw_up, raw_down = gz < nz - 2, gz > 1
    near_top, near_bottom = gz == nz - 2, gz == 1
    near = near_top | near_bottom
    at_end = jnp.logical_not(inside)
    middle = inside & jnp.logical_not(near)
    beside_end = jnp.where(near_top, gz + 1, gz - 1)
    inward = jnp.where(has_below, gz - 1, gz + 1)

    def remote(src, dst, send, recv, **where):
        return pltpu.make_async_remote_copy(
            src_ref=src, dst_ref=dst, send_sem=send, recv_sem=recv, device_id=where, device_id_type=MESH
        )

    def load(f, h):
        columns = pl.ds(pl.multiple_of(h * lanes, lanes), lanes)
        return pltpu.make_async_copy(
            green.at[:, :, f, :, :, columns], own.at[f, gz, h], load_sem.at[f, h]
        )

    def z_up(f, slab, h):
        here = own.at[f, slab, h]
        return remote(here, here, send_zu.at[f, slab, h], own_sem.at[f, slab, h], sa=gz + 1)

    def z_down(f, slab, h):
        here = own.at[f, slab, h]
        return remote(here, here, send_zd.at[f, slab, h], own_sem.at[f, slab, h], sa=gz - 1)

    def y_down(f, slab, h):
        return remote(
            own.at[f, slab, h, :, 0], up.at[f, slab, h],
            send_yd.at[f, slab, h], up_sem.at[f, slab, h], gy=gy - 1,
        )

    def y_up(f, slab, h):
        return remote(
            own.at[f, slab, h, :, tiles_y - 1], down.at[f, slab, h],
            send_yu.at[f, slab, h], down_sem.at[f, slab, h], gy=gy + 1,
        )

    def x_left(kind, f, slab, h):
        src, dst = (
            (own.at[f, slab, h, 0], right.at[f, slab, h, pl.ds(1, tiles_y)]),
            (up.at[f, slab, h, 0], right.at[f, slab, h, tiles_y + 1]),
            (down.at[f, slab, h, 0], right.at[f, slab, h, 0]),
        )[kind]
        return remote(
            src, dst, send_x.at[kind, f, slab, h], right_sem.at[kind, f, slab, h], gx=gx - 1
        )

    def to_end(f, h, part):
        columns = pl.ds(pl.multiple_of(part * points + h * lanes, lanes), lanes)
        return remote(
            stage.at[:, :, :, f, :, columns], out.at[:, :, :, f, :, columns],
            send_end.at[f, h, part], end_sem.at[f, h, part], sa=beside_end,
        )

    def halo_up(f, h):
        here = up.at[f, gz, h]
        return remote(here, here, send_halo.at[0, f, h], up_sem.at[f, gz, h], sa=inward)

    def halo_down(f, h):
        here = down.at[f, gz, h]
        return remote(here, here, send_halo.at[1, f, h], down_sem.at[f, gz, h], sa=inward)

    def each(count, body, start=0):
        def step(i, carry):
            body(i)
            return carry

        lax.fori_loop(start, count, step, 0)

    def each_half(body):
        each(phases, lambda u: body(u // halves, u % halves))

    each_half(lambda f, h: load(f, h).start())

    barrier = pltpu.get_barrier_semaphore()
    sides = (
        (has_above, dict(sa=gz + 1)), (has_below, dict(sa=gz - 1)),
        (has_up, dict(gy=gy + 1)), (has_down, dict(gy=gy - 1)),
        (has_right, dict(gx=gx + 1)), (has_left, dict(gx=gx - 1)),
    )
    for there, where in sides:
        @pl.when(there)
        def _():
            pl.semaphore_signal(barrier, inc=1, device_id=where, device_id_type=MESH)
    pl.semaphore_wait(barrier, sum(there.astype(jnp.int32) for there, _ in sides))

    def push_x(f, slab, h):
        pl.when(has_left)(lambda: x_left(0, f, slab, h).start())

    def push(f, slab, h):
        pl.when(has_down)(lambda: y_down(f, slab, h).start())
        pl.when(has_up)(lambda: y_up(f, slab, h).start())
        push_x(f, slab, h)

    def halo_y(f, slab, h):
        @pl.when(has_up)
        def _():
            y_down(f, slab, h).wait_recv()
            pl.when(has_left)(lambda: x_left(1, f, slab, h).start())

        @pl.when(has_down)
        def _():
            y_up(f, slab, h).wait_recv()
            pl.when(has_left)(lambda: x_left(2, f, slab, h).start())

    def halo_x(f, slab, h):
        @pl.when(has_right)
        def _():
            x_left(0, f, slab, h).wait_recv()
            pl.when(has_up)(lambda: x_left(1, f, slab, h).wait_recv())
            pl.when(has_down)(lambda: x_left(2, f, slab, h).wait_recv())

    def send_own(u):
        f, v = u // halves, u % halves
        pl.when(raw_up)(lambda: z_up(f, gz, 1 - v).start())
        pl.when(raw_down)(lambda: z_down(f, gz, v).start())

    mine = gz * width // lanes
    row_at = pl.multiple_of(gz * width % lanes, width)
    row_beyond = pl.multiple_of(beside_end * width % lanes, width)

    def products(f, slab, h, both):
        rows = 4 * width if both else 2 * width
        for tx in range(tiles_x):
            for ty in range(tiles_y):
                for part in range(2):
                    turned[part] = own[f, slab, mine, tx, ty, part].T
                for base, start in ((0, row_at), (2 * width, row_beyond))[: 2 if both else 1]:
                    real = turned[0, pl.ds(start, width), :]
                    imag = turned[1, pl.ds(start, width), :]
                    left[base : base + width, :traces] = real
                    left[base : base + width, traces:] = imag
                    left[base + width : base + 2 * width, :traces] = -imag
                    left[base + width : base + 2 * width, traces:] = real
                def tile(ox, oy):
                    if ox == tiles_x:
                        return right.at[f, slab, h, oy + 1]
                    if oy == tiles_y:
                        return up.at[f, slab, h, ox]
                    if oy < 0:
                        return down.at[f, slab, h, ox]
                    return own.at[f, slab, h, ox, oy]

                def add(group):
                    beside = [
                        tile(tx + CANDIDATES[c][0], ty + CANDIDATES[c][1])[...].reshape(2 * traces, lanes)
                        for c in group
                    ]
                    blocks = jnp.dot(
                        left[:rows], jnp.concatenate(beside, axis=1) if len(group) > 1 else beside[0],
                        preferred_element_type=jnp.float32,
                    )
                    for i, c in enumerate(group):
                        block = blocks[:, i * lanes : (i + 1) * lanes]
                        total[f, tx, ty, c, h, :, :lanes] += block[:width]
                        total[f, tx, ty, c, h, :, lanes:] += block[width : 2 * width]
                        if both:
                            beyond[f, tx, ty, c, h, :, :lanes] += block[2 * width : 3 * width]
                            beyond[f, tx, ty, c, h, :, lanes:] += block[3 * width :]

                def run(group, there):
                    if there is True:
                        add(group)
                    else:
                        pl.when(there)(lambda: add(group))

                for group in GROUPS:
                    oy = ty + CANDIDATES[group[0]][1]
                    there = has_up if oy == tiles_y else has_down if oy < 0 else True
                    if tx + 1 < tiles_x:
                        run(group, there)
                        continue
                    near_ones = tuple(c for c in group if CANDIDATES[c][0] == 0)
                    run(group, has_right if there is True else there & has_right)
                    if near_ones:
                        alone = jnp.logical_not(has_right)
                        run(near_ones, alone if there is True else there & alone)

    def choose(f, h, source, target, add):
        for k in range(pairs):
            wanted = offsets[1, k] + 3 * offsets[0, k]
            for tx in range(tiles_x):
                for ty in range(tiles_y):
                    for part in range(2):
                        columns = pl.ds(pl.multiple_of(part * points + h * lanes, lanes), lanes)
                        value = source[f, tx, ty, wanted, h, :, part * lanes : (part + 1) * lanes]
                        if add:
                            value = value + target[tx, ty, k, f, :, columns]
                        target[tx, ty, k, f, :, columns] = value

    def rest(f, slab):
        each(halves, lambda h: halo_y(f, slab, h))

        def part(h):
            halo_x(f, slab, h)
            products(f, slab, h, False)

        each(halves, part)

    each(halves, lambda h: load(0, h).wait())
    send_own(0)

    @pl.when(near)
    def _():
        push(0, gz, jnp.where(near_top, 1, 0))

    each(phases, lambda u: load(u // halves, u % halves).wait(), halves)

    @pl.when(at_end)
    def _():
        send_own(1)
        each_half(lambda f, v: push(f, gz, jnp.where(gz == 0, v, 1 - v)))
        total[...] = jnp.zeros_like(total)

        def pass_halo(f, v):
            h = jnp.where(gz == 0, v, 1 - v)
            halo_y(f, gz, h)
            pl.when(has_up)(lambda: halo_up(f, h).start())
            pl.when(has_down)(lambda: halo_down(f, h).start())
            u = f * halves + v
            pl.when(u + 2 < phases)(lambda: send_own(u + 2))

        each_half(pass_halo)

        def own_part(f, h):
            halo_x(f, gz, h)
            products(f, gz, h, False)

        each_half(own_part)

        def receive(f, v):
            h = jnp.where(gz == 0, v, 1 - v)
            for part in range(2):
                to_end(f, h, part).wait_recv()
            choose(f, h, total, out, True)

        each_half(receive)

    @pl.when(near)
    def _():
        end = beside_end

        def pass_end(u):
            f, v = u // halves, u % halves

            @pl.when(near_top)
            def _():
                z_down(f, end, v).wait_recv()
                z_down(f, end, v).start()
                push_x(f, end, v)

            @pl.when(near_bottom)
            def _():
                z_up(f, end, 1 - v).wait_recv()
                z_up(f, end, 1 - v).start()
                push_x(f, end, 1 - v)

            pl.when(u + 1 < phases)(lambda: send_own(u + 1))

        total[...] = jnp.zeros_like(total)
        beyond[...] = jnp.zeros_like(beyond)

        def near_half(v):
            return jnp.where(near_top, 1 - v, v)

        def work(f, slab, h):
            halo_x(f, slab, h)
            products(f, slab, h, True)

        halo_y(0, gz, near_half(0))
        work(0, gz, near_half(0))
        pass_end(0)

        def rest_half(f, v):
            h = jnp.where(near_top, v, 1 - v)
            halo_y(f, end, h)
            halo_x(f, end, h)
            products(f, end, h, False)

        def phase(f, v):
            u = f * halves + v
            more = u + 1 < phases
            h = near_half(v)
            next_f, next_h = (u + 1) // halves, near_half((u + 1) % halves)

            def at(d):
                slab = jnp.where(near_top, gz - d, gz + d)

                @pl.when(near_top)
                def _():
                    z_up(f, slab, h).wait_recv()

                @pl.when(near_bottom)
                def _():
                    z_down(f, slab, h).wait_recv()

                push(f, slab, h)
                pl.when((d == 1) & more)(lambda: push(next_f, gz, next_h))
                pl.when((d == 2) & more)(lambda: pass_end(u + 1))
                pl.when((d == 1) & (f > 0))(lambda: rest_half(f - 1, v))
                first = jnp.where((d == 2) & more, 0, 1)

                def one(i):
                    own_turn = i == 0
                    pl.when(i == 1)(lambda: halo_y(f, slab, h))
                    work(
                        jnp.where(own_turn, next_f, f),
                        jnp.where(own_turn, gz, slab),
                        jnp.where(own_turn, next_h, h),
                    )

                each(2, one, first)
                pl.when((d == 1) & more)(lambda: halo_y(next_f, gz, next_h))

            each(nz - 1, at, 1)
            choose(f, h, beyond, stage, False)
            for part in range(2):
                to_end(f, h, part).start()

            @pl.when((v == halves - 1) & (f > 0))
            def _():
                each(halves, lambda i: choose(f - 1, i, total, out, False))

        each_half(phase)
        each(halves, lambda v: rest_half(freqs - 1, v))
        each(halves, lambda h: choose(freqs - 1, h, total, out, False))

    if nz > 4:
        @pl.when(middle)
        def _():
            each_half(lambda f, h: push(f, gz, h))
            total[...] = jnp.zeros_like(total)

            def phase(f, v):
                u = f * halves + v

                def at(d):
                    lower, upper = gz - d, gz + d

                    @pl.when(lower >= 0)
                    def _():
                        z_up(f, lower, 1 - v).wait_recv()
                        z_up(f, lower, 1 - v).start()
                        push(f, lower, 1 - v)

                    @pl.when(upper < nz)
                    def _():
                        z_down(f, upper, v).wait_recv()
                        z_down(f, upper, v).start()
                        push(f, upper, v)

                    pl.when((d == 1) & (u + 1 < phases))(lambda: send_own(u + 1))

                each(nz, at, 1)

                @pl.when(v == halves - 1)
                def _():
                    each(nz, lambda slab: rest(f, slab))
                    each(halves, lambda h: choose(f, h, total, out, False))

            each_half(phase)

    def finish(slab):
        def body(f, h):
            pl.when(raw_up & (slab <= gz))(lambda: z_up(f, slab, h).wait_send())
            pl.when(raw_down & (slab >= gz))(lambda: z_down(f, slab, h).wait_send())

            @pl.when(middle | (slab == gz) | (near & (slab != beside_end)))
            def _():
                pl.when(has_down)(lambda: y_down(f, slab, h).wait_send())
                pl.when(has_up)(lambda: y_up(f, slab, h).wait_send())

            @pl.when(at_end & (slab == gz))
            def _():
                pl.when(has_up)(lambda: halo_up(f, h).wait_send())
                pl.when(has_down)(lambda: halo_down(f, h).wait_send())

            @pl.when(inside | (slab == gz))
            def _():

                @pl.when(has_left)
                def _():
                    x_left(0, f, slab, h).wait_send()
                    pl.when(has_up)(lambda: x_left(1, f, slab, h).wait_send())
                    pl.when(has_down)(lambda: x_left(2, f, slab, h).wait_send())

        each_half(body)

    each(nz, finish)

    @pl.when(near)
    def _():
        def body(f, h):
            for part in range(2):
                to_end(f, h, part).wait_send()

        each_half(body)


def per_device(green, offsets):
    tiles_x, tiles_y, freqs, _, traces, points = green.shape
    nx, ny, nz = (lax.axis_size(name) for name in ("gx", "gy", "sa"))
    width, lanes, pairs = points // nz, 128, offsets.shape[0]
    halves = points // lanes
    dma = pltpu.SemaphoreType.DMA
    result = (tiles_x, tiles_y, pairs, freqs, width, 2 * points)
    sums = (freqs, tiles_x, tiles_y, len(CANDIDATES), halves, width, 2 * lanes)
    piece, cell = (freqs, nz, halves), (2, traces, lanes)
    return pl.pallas_call(
        functools.partial(kernel, nx, ny, nz),
        out_shape=jax.ShapeDtypeStruct(result, jnp.float32),
        in_specs=[pl.BlockSpec(memory_space=pl.ANY), pl.BlockSpec(memory_space=pltpu.SMEM)],
        out_specs=pl.BlockSpec(memory_space=pltpu.VMEM),
        scratch_shapes=[
            pltpu.VMEM(sums, jnp.float32),
            pltpu.VMEM(sums, jnp.float32),
            pltpu.VMEM(result, jnp.float32),
            pltpu.VMEM(piece + (tiles_x, tiles_y) + cell, jnp.bfloat16),
            pltpu.VMEM(piece + (tiles_x,) + cell, jnp.bfloat16),
            pltpu.VMEM(piece + (tiles_x,) + cell, jnp.bfloat16),
            pltpu.VMEM(piece + (tiles_y + 2,) + cell, jnp.bfloat16),
            pltpu.VMEM((2, lanes, traces), jnp.bfloat16),
            pltpu.VMEM((4 * width, 2 * traces), jnp.bfloat16),
            dma((freqs, halves)),
            dma(piece),
            dma(piece),
            dma(piece),
            dma((3,) + piece),
            dma((freqs, halves, 2)),
            dma(piece),
            dma(piece),
            dma(piece),
            dma(piece),
            dma((3,) + piece),
            dma((freqs, halves, 2)),
            dma((2, freqs, halves)),
        ],
        compiler_params=pltpu.CompilerParams(
            collective_id=0, has_side_effects=True, vmem_limit_bytes=61 * 2**20
        ),
        cost_estimate=pl.CostEstimate(
            flops=2 * tiles_x * tiles_y * freqs * len(CANDIDATES) * width * 2 * points * 2 * traces * nz,
            bytes_accessed=12 * 2**20, transcendentals=0,
        ),
    )(green, offsets.T)


def solution(mesh):
    return jax.shard_map(
        per_device,
        mesh=mesh,
        in_specs=(P("gx", "gy", None, None, "sa", None), P()),
        out_specs=P("gx", "gy", None, None, "sa", None),
        check_vma=False,
    )
```

```python
import functools

import jax
import jax.numpy as jnp
from jax import lax
from jax.experimental import pallas as pl
from jax.experimental.pallas import tpu as pltpu
from jax.sharding import PartitionSpec as P

MESH = pl.DeviceIdType.MESH
CANDIDATES = ((0, 0), (0, 1), (1, -1), (1, 0), (1, 1))
GROUPS = ((0, 3), (1, 4), (2,))


def kernel(
    nx, ny, nz, green, offsets, out, total, beyond, stage, own, up, down, right, turned, left,
    load_sem, own_sem, up_sem, down_sem, right_sem, end_sem,
    send_zu, send_zd, send_yu, send_yd, send_x, send_end, send_halo,
):
    freqs, _, halves, tiles_x, tiles_y, _, traces, lanes = own.shape
    points = halves * lanes
    width = points // nz
    phases = halves * freqs
    pairs = offsets.shape[1]
    gx, gy, gz = lax.axis_index("gx"), lax.axis_index("gy"), lax.axis_index("sa")
    has_right, has_left = gx < nx - 1, gx > 0
    has_up, has_down = gy < ny - 1, gy > 0
    has_above, has_below = gz < nz - 1, gz > 0
    inside = has_above & has_below
    raw_up, raw_down = gz < nz - 2, gz > 1
    near_top, near_bottom = gz == nz - 2, gz == 1
    near = near_top | near_bottom
    at_end = jnp.logical_not(inside)
    middle = inside & jnp.logical_not(near)
    beside_end = jnp.where(near_top, gz + 1, gz - 1)
    inward = jnp.where(has_below, gz - 1, gz + 1)

    def remote(src, dst, send, recv, **where):
        return pltpu.make_async_remote_copy(
            src_ref=src, dst_ref=dst, send_sem=send, recv_sem=recv, device_id=where, device_id_type=MESH
        )

    def load(f, h):
        columns = pl.ds(pl.multiple_of(h * lanes, lanes), lanes)
        return pltpu.make_async_copy(
            green.at[:, :, f, :, :, columns], own.at[f, gz, h], load_sem.at[f, h]
        )

    def z_up(f, slab, h):
        here = own.at[f, slab, h]
        return remote(here, here, send_zu.at[f, slab, h], own_sem.at[f, slab, h], sa=gz + 1)

    def z_down(f, slab, h):
        here = own.at[f, slab, h]
        return remote(here, here, send_zd.at[f, slab, h], own_sem.at[f, slab, h], sa=gz - 1)

    def y_down(f, slab, h, tx):
        return remote(
            own.at[f, slab, h, tx, 0], up.at[f, slab, h, tx],
            send_yd.at[f, slab, h, tx], up_sem.at[f, slab, h, tx], gy=gy - 1,
        )

    def y_up(f, slab, h, tx):
        return remote(
            own.at[f, slab, h, tx, tiles_y - 1], down.at[f, slab, h, tx],
            send_yu.at[f, slab, h, tx], down_sem.at[f, slab, h, tx], gy=gy + 1,
        )

    def x_left(kind, f, slab, h):
        src, dst = (
            (own.at[f, slab, h, 0], right.at[f, slab, h, pl.ds(1, tiles_y)]),
            (up.at[f, slab, h, 0], right.at[f, slab, h, tiles_y + 1]),
            (down.at[f, slab, h, 0], right.at[f, slab, h, 0]),
        )[kind]
        return remote(
            src, dst, send_x.at[kind, f, slab, h], right_sem.at[kind, f, slab, h], gx=gx - 1
        )

    def to_end(f, h, part):
        columns = pl.ds(pl.multiple_of(part * points + h * lanes, lanes), lanes)
        return remote(
            stage.at[:, :, :, f, :, columns], out.at[:, :, :, f, :, columns],
            send_end.at[f, h, part], end_sem.at[f, h, part], sa=beside_end,
        )

    def halo_up(f, h, tx):
        here = up.at[f, gz, h, tx]
        return remote(here, here, send_halo.at[0, f, h, tx], up_sem.at[f, gz, h, tx], sa=inward)

    def halo_down(f, h, tx):
        here = down.at[f, gz, h, tx]
        return remote(here, here, send_halo.at[1, f, h, tx], down_sem.at[f, gz, h, tx], sa=inward)

    def each(count, body, start=0):
        def step(i, carry):
            body(i)
            return carry

        lax.fori_loop(start, count, step, 0)

    def each_half(body):
        each(phases, lambda u: body(u // halves, u % halves))

    each_half(lambda f, h: load(f, h).start())

    barrier = pltpu.get_barrier_semaphore()
    sides = (
        (has_above, dict(sa=gz + 1)), (has_below, dict(sa=gz - 1)),
        (has_up, dict(gy=gy + 1)), (has_down, dict(gy=gy - 1)),
        (has_right, dict(gx=gx + 1)), (has_left, dict(gx=gx - 1)),
    )
    for there, where in sides:
        @pl.when(there)
        def _():
            pl.semaphore_signal(barrier, inc=1, device_id=where, device_id_type=MESH)
    pl.semaphore_wait(barrier, sum(there.astype(jnp.int32) for there, _ in sides))

    def push_x(f, slab, h):
        pl.when(has_left)(lambda: x_left(0, f, slab, h).start())

    def push(f, slab, h):
        push_x(f, slab, h)
        for tx in range(tiles_x):
            pl.when(has_down)(lambda: y_down(f, slab, h, tx).start())
            pl.when(has_up)(lambda: y_up(f, slab, h, tx).start())

    def halo_y(f, slab, h):
        for tx in range(tiles_x):
            @pl.when(has_up)
            def _():
                y_down(f, slab, h, tx).wait_recv()
                if tx == 0:
                    pl.when(has_left)(lambda: x_left(1, f, slab, h).start())

            @pl.when(has_down)
            def _():
                y_up(f, slab, h, tx).wait_recv()
                if tx == 0:
                    pl.when(has_left)(lambda: x_left(2, f, slab, h).start())

    def halo_x(f, slab, h):
        @pl.when(has_right)
        def _():
            x_left(0, f, slab, h).wait_recv()
            pl.when(has_up)(lambda: x_left(1, f, slab, h).wait_recv())
            pl.when(has_down)(lambda: x_left(2, f, slab, h).wait_recv())

    def send_own(u):
        f, v = u // halves, u % halves
        pl.when(raw_up)(lambda: z_up(f, gz, 1 - v).start())
        pl.when(raw_down)(lambda: z_down(f, gz, v).start())

    mine = gz * width // lanes
    row_at = pl.multiple_of(gz * width % lanes, width)
    row_beyond = pl.multiple_of(beside_end * width % lanes, width)

    def products(f, slab, h, both):
        rows = 4 * width if both else 2 * width
        for tx in range(tiles_x):
            for ty in range(tiles_y):
                for part in range(2):
                    turned[part] = own[f, slab, mine, tx, ty, part].T
                for base, start in ((0, row_at), (2 * width, row_beyond))[: 2 if both else 1]:
                    real = turned[0, pl.ds(start, width), :]
                    imag = turned[1, pl.ds(start, width), :]
                    left[base : base + width, :traces] = real
                    left[base : base + width, traces:] = imag
                    left[base + width : base + 2 * width, :traces] = -imag
                    left[base + width : base + 2 * width, traces:] = real
                def tile(ox, oy):
                    if ox == tiles_x:
                        return right.at[f, slab, h, oy + 1]
                    if oy == tiles_y:
                        return up.at[f, slab, h, ox]
                    if oy < 0:
                        return down.at[f, slab, h, ox]
                    return own.at[f, slab, h, ox, oy]

                def add(group):
                    beside = [
                        tile(tx + CANDIDATES[c][0], ty + CANDIDATES[c][1])[...].reshape(2 * traces, lanes)
                        for c in group
                    ]
                    blocks = jnp.dot(
                        left[:rows], jnp.concatenate(beside, axis=1) if len(group) > 1 else beside[0],
                        preferred_element_type=jnp.float32,
                    )
                    for i, c in enumerate(group):
                        block = blocks[:, i * lanes : (i + 1) * lanes]
                        total[f, tx, ty, c, h, :, :lanes] += block[:width]
                        total[f, tx, ty, c, h, :, lanes:] += block[width : 2 * width]
                        if both:
                            beyond[f, tx, ty, c, h, :, :lanes] += block[2 * width : 3 * width]
                            beyond[f, tx, ty, c, h, :, lanes:] += block[3 * width :]

                def run(group, there):
                    if there is True:
                        add(group)
                    else:
                        pl.when(there)(lambda: add(group))

                for group in GROUPS:
                    oy = ty + CANDIDATES[group[0]][1]
                    there = has_up if oy == tiles_y else has_down if oy < 0 else True
                    if tx + 1 < tiles_x:
                        run(group, there)
                        continue
                    near_ones = tuple(c for c in group if CANDIDATES[c][0] == 0)
                    run(group, has_right if there is True else there & has_right)
                    if near_ones:
                        alone = jnp.logical_not(has_right)
                        run(near_ones, alone if there is True else there & alone)

    def choose(f, h, source, target, add):
        for k in range(pairs):
            wanted = offsets[1, k] + 3 * offsets[0, k]
            for tx in range(tiles_x):
                for ty in range(tiles_y):
                    for part in range(2):
                        columns = pl.ds(pl.multiple_of(part * points + h * lanes, lanes), lanes)
                        value = source[f, tx, ty, wanted, h, :, part * lanes : (part + 1) * lanes]
                        if add:
                            value = value + target[tx, ty, k, f, :, columns]
                        target[tx, ty, k, f, :, columns] = value

    def rest(f, slab):
        each(halves, lambda h: halo_y(f, slab, h))

        def part(h):
            halo_x(f, slab, h)
            products(f, slab, h, False)

        each(halves, part)

    each(halves, lambda h: load(0, h).wait())
    send_own(0)

    @pl.when(near)
    def _():
        push(0, gz, jnp.where(near_top, 1, 0))

    each(phases, lambda u: load(u // halves, u % halves).wait(), halves)

    @pl.when(at_end)
    def _():
        send_own(1)
        each_half(lambda f, v: push(f, gz, jnp.where(gz == 0, v, 1 - v)))
        total[...] = jnp.zeros_like(total)

        def pass_halo(f, v):
            h = jnp.where(gz == 0, v, 1 - v)
            halo_y(f, gz, h)
            for tx in range(tiles_x):
                pl.when(has_up)(lambda: halo_up(f, h, tx).start())
                pl.when(has_down)(lambda: halo_down(f, h, tx).start())
            u = f * halves + v
            pl.when(u + 2 < phases)(lambda: send_own(u + 2))

        each_half(pass_halo)

        def own_part(f, h):
            halo_x(f, gz, h)
            products(f, gz, h, False)

        each_half(own_part)

        def receive(f, v):
            h = jnp.where(gz == 0, v, 1 - v)
            for part in range(2):
                to_end(f, h, part).wait_recv()
            choose(f, h, total, out, True)

        each_half(receive)

    @pl.when(near)
    def _():
        end = beside_end

        def pass_end(u):
            f, v = u // halves, u % halves

            @pl.when(near_top)
            def _():
                z_down(f, end, v).wait_recv()
                z_down(f, end, v).start()

            @pl.when(near_bottom)
            def _():
                z_up(f, end, 1 - v).wait_recv()
                z_up(f, end, 1 - v).start()

            pl.when(u + 1 < phases)(lambda: send_own(u + 1))

        total[...] = jnp.zeros_like(total)
        beyond[...] = jnp.zeros_like(beyond)

        def near_half(v):
            return jnp.where(near_top, 1 - v, v)

        def work(f, slab, h):
            halo_x(f, slab, h)
            products(f, slab, h, True)

        halo_y(0, gz, near_half(0))
        work(0, gz, near_half(0))
        pass_end(0)
        push_x(0, end, jnp.where(near_top, 0, 1))

        def rest_half(f, v):
            h = jnp.where(near_top, v, 1 - v)
            halo_y(f, end, h)
            halo_x(f, end, h)
            products(f, end, h, False)

        def phase(f, v):
            u = f * halves + v
            more = u + 1 < phases
            h = near_half(v)
            next_f, next_h = (u + 1) // halves, near_half((u + 1) % halves)

            def at(d):
                slab = jnp.where(near_top, gz - d, gz + d)

                @pl.when(near_top)
                def _():
                    z_up(f, slab, h).wait_recv()

                @pl.when(near_bottom)
                def _():
                    z_down(f, slab, h).wait_recv()

                push(f, slab, h)
                pl.when((d == 2) & more)(lambda: pass_end(u + 1))
                pl.when((d == 1) & (f > 0))(lambda: rest_half(f - 1, v))
                first = jnp.where((d == 2) & more, 0, 1)

                def one(i):
                    own_turn = i == 0

                    @pl.when(i == 1)
                    def _():
                        halo_y(f, slab, h)
                        pl.when((d == 1) & more)(lambda: push(next_f, gz, next_h))
                        pl.when((d == 2) & more)(
                            lambda: push_x(next_f, end, jnp.where(near_top, (u + 1) % halves, 1 - (u + 1) % halves))
                        )

                    work(
                        jnp.where(own_turn, next_f, f),
                        jnp.where(own_turn, gz, slab),
                        jnp.where(own_turn, next_h, h),
                    )

                each(2, one, first)
                pl.when((d == 1) & more)(lambda: halo_y(next_f, gz, next_h))

            each(nz - 1, at, 1)
            choose(f, h, beyond, stage, False)
            for part in range(2):
                to_end(f, h, part).start()

            @pl.when((v == halves - 1) & (f > 0))
            def _():
                each(halves, lambda i: choose(f - 1, i, total, out, False))

        each_half(phase)
        each(halves, lambda v: rest_half(freqs - 1, v))
        each(halves, lambda h: choose(freqs - 1, h, total, out, False))

    if nz > 4:
        @pl.when(middle)
        def _():
            each_half(lambda f, h: push(f, gz, h))
            total[...] = jnp.zeros_like(total)

            def phase(f, v):
                u = f * halves + v

                def at(d):
                    lower, upper = gz - d, gz + d

                    @pl.when(lower >= 0)
                    def _():
                        z_up(f, lower, 1 - v).wait_recv()
                        z_up(f, lower, 1 - v).start()
                        push(f, lower, 1 - v)

                    @pl.when(upper < nz)
                    def _():
                        z_down(f, upper, v).wait_recv()
                        z_down(f, upper, v).start()
                        push(f, upper, v)

                    pl.when((d == 1) & (u + 1 < phases))(lambda: send_own(u + 1))

                each(nz, at, 1)

                @pl.when(v == halves - 1)
                def _():
                    each(nz, lambda slab: rest(f, slab))
                    each(halves, lambda h: choose(f, h, total, out, False))

            each_half(phase)

    def finish(slab):
        def body(f, h):
            pl.when(raw_up & (slab <= gz))(lambda: z_up(f, slab, h).wait_send())
            pl.when(raw_down & (slab >= gz))(lambda: z_down(f, slab, h).wait_send())

            @pl.when(middle | (slab == gz) | (near & (slab != beside_end)))
            def _():
                for tx in range(tiles_x):
                    pl.when(has_down)(lambda: y_down(f, slab, h, tx).wait_send())
                    pl.when(has_up)(lambda: y_up(f, slab, h, tx).wait_send())

            @pl.when(at_end & (slab == gz))
            def _():
                for tx in range(tiles_x):
                    pl.when(has_up)(lambda: halo_up(f, h, tx).wait_send())
                    pl.when(has_down)(lambda: halo_down(f, h, tx).wait_send())

            @pl.when(inside | (slab == gz))
            def _():

                @pl.when(has_left)
                def _():
                    x_left(0, f, slab, h).wait_send()
                    pl.when(has_up)(lambda: x_left(1, f, slab, h).wait_send())
                    pl.when(has_down)(lambda: x_left(2, f, slab, h).wait_send())

        each_half(body)

    each(nz, finish)

    @pl.when(near)
    def _():
        def body(f, h):
            for part in range(2):
                to_end(f, h, part).wait_send()

        each_half(body)


def per_device(green, offsets):
    tiles_x, tiles_y, freqs, _, traces, points = green.shape
    nx, ny, nz = (lax.axis_size(name) for name in ("gx", "gy", "sa"))
    width, lanes, pairs = points // nz, 128, offsets.shape[0]
    halves = points // lanes
    dma = pltpu.SemaphoreType.DMA
    result = (tiles_x, tiles_y, pairs, freqs, width, 2 * points)
    sums = (freqs, tiles_x, tiles_y, len(CANDIDATES), halves, width, 2 * lanes)
    piece, cell = (freqs, nz, halves), (2, traces, lanes)
    return pl.pallas_call(
        functools.partial(kernel, nx, ny, nz),
        out_shape=jax.ShapeDtypeStruct(result, jnp.float32),
        in_specs=[pl.BlockSpec(memory_space=pl.ANY), pl.BlockSpec(memory_space=pltpu.SMEM)],
        out_specs=pl.BlockSpec(memory_space=pltpu.VMEM),
        scratch_shapes=[
            pltpu.VMEM(sums, jnp.float32),
            pltpu.VMEM(sums, jnp.float32),
            pltpu.VMEM(result, jnp.float32),
            pltpu.VMEM(piece + (tiles_x, tiles_y) + cell, jnp.bfloat16),
            pltpu.VMEM(piece + (tiles_x,) + cell, jnp.bfloat16),
            pltpu.VMEM(piece + (tiles_x,) + cell, jnp.bfloat16),
            pltpu.VMEM(piece + (tiles_y + 2,) + cell, jnp.bfloat16),
            pltpu.VMEM((2, lanes, traces), jnp.bfloat16),
            pltpu.VMEM((4 * width, 2 * traces), jnp.bfloat16),
            dma((freqs, halves)),
            dma(piece),
            dma(piece + (tiles_x,)),
            dma(piece + (tiles_x,)),
            dma((3,) + piece),
            dma((freqs, halves, 2)),
            dma(piece),
            dma(piece),
            dma(piece + (tiles_x,)),
            dma(piece + (tiles_x,)),
            dma((3,) + piece),
            dma((freqs, halves, 2)),
            dma((2, freqs, halves, tiles_x)),
        ],
        compiler_params=pltpu.CompilerParams(
            collective_id=0, has_side_effects=True, vmem_limit_bytes=61 * 2**20
        ),
        cost_estimate=pl.CostEstimate(
            flops=2 * tiles_x * tiles_y * freqs * len(CANDIDATES) * width * 2 * points * 2 * traces * nz,
            bytes_accessed=12 * 2**20, transcendentals=0,
        ),
    )(green, offsets.T)


def solution(mesh):
    return jax.shard_map(
        per_device,
        mesh=mesh,
        in_specs=(P("gx", "gy", None, None, "sa", None), P()),
        out_specs=P("gx", "gy", None, None, "sa", None),
        check_vma=False,
    )
```

```python
import functools

import jax
import jax.numpy as jnp
from jax import lax
from jax.experimental import pallas as pl
from jax.experimental.pallas import tpu as pltpu
from jax.sharding import PartitionSpec as P

MESH = pl.DeviceIdType.MESH
CANDIDATES = ((0, 0), (0, 1), (1, -1), (1, 0), (1, 1))
GROUPS = ((0, 3), (1, 4), (2,))


def kernel(
    nx, ny, nz, green, offsets, out, total, beyond, stage, own, up, down, right, turned, left,
    load_sem, own_sem, up_sem, down_sem, right_sem, end_sem,
    send_zu, send_zd, send_yu, send_yd, send_x, send_end, send_halo,
):
    freqs, _, halves, tiles_x, tiles_y, _, traces, lanes = own.shape
    points = halves * lanes
    width = points // nz
    phases = halves * freqs
    pairs = offsets.shape[1]
    gx, gy, gz = lax.axis_index("gx"), lax.axis_index("gy"), lax.axis_index("sa")
    has_right, has_left = gx < nx - 1, gx > 0
    has_up, has_down = gy < ny - 1, gy > 0
    has_above, has_below = gz < nz - 1, gz > 0
    inside = has_above & has_below
    raw_up, raw_down = gz < nz - 2, gz > 1
    near_top, near_bottom = gz == nz - 2, gz == 1
    near = near_top | near_bottom
    at_end = jnp.logical_not(inside)
    middle = inside & jnp.logical_not(near)
    beside_end = jnp.where(near_top, gz + 1, gz - 1)
    inward = jnp.where(has_below, gz - 1, gz + 1)

    def remote(src, dst, send, recv, **where):
        return pltpu.make_async_remote_copy(
            src_ref=src, dst_ref=dst, send_sem=send, recv_sem=recv, device_id=where, device_id_type=MESH
        )

    def load(f, h):
        columns = pl.ds(pl.multiple_of(h * lanes, lanes), lanes)
        return pltpu.make_async_copy(
            green.at[:, :, f, :, :, columns], own.at[f, gz, h], load_sem.at[f, h]
        )

    def z_up(f, slab, h):
        here = own.at[f, slab, h]
        return remote(here, here, send_zu.at[f, slab, h], own_sem.at[f, slab, h], sa=gz + 1)

    def z_down(f, slab, h):
        here = own.at[f, slab, h]
        return remote(here, here, send_zd.at[f, slab, h], own_sem.at[f, slab, h], sa=gz - 1)

    def y_down(f, slab, h):
        return remote(
            own.at[f, slab, h, :, 0], up.at[f, slab, h],
            send_yd.at[f, slab, h], up_sem.at[f, slab, h], gy=gy - 1,
        )

    def y_up(f, slab, h):
        return remote(
            own.at[f, slab, h, :, tiles_y - 1], down.at[f, slab, h],
            send_yu.at[f, slab, h], down_sem.at[f, slab, h], gy=gy + 1,
        )

    def x_left(kind, f, slab, h):
        src, dst = (
            (own.at[f, slab, h, 0], right.at[f, slab, h, pl.ds(1, tiles_y)]),
            (up.at[f, slab, h, 0], right.at[f, slab, h, tiles_y + 1]),
            (down.at[f, slab, h, 0], right.at[f, slab, h, 0]),
        )[kind]
        return remote(
            src, dst, send_x.at[kind, f, slab, h], right_sem.at[kind, f, slab, h], gx=gx - 1
        )

    def to_end(f, h, part):
        columns = pl.ds(pl.multiple_of(part * points + h * lanes, lanes), lanes)
        return remote(
            stage.at[:, :, :, f, :, columns], out.at[:, :, :, f, :, columns],
            send_end.at[f, h, part], end_sem.at[f, h, part], sa=beside_end,
        )

    def halo_up(f, h):
        here = up.at[f, gz, h]
        return remote(here, here, send_halo.at[0, f, h], up_sem.at[f, gz, h], sa=inward)

    def halo_down(f, h):
        here = down.at[f, gz, h]
        return remote(here, here, send_halo.at[1, f, h], down_sem.at[f, gz, h], sa=inward)

    def each(count, body, start=0):
        def step(i, carry):
            body(i)
            return carry

        lax.fori_loop(start, count, step, 0)

    def each_half(body):
        each(phases, lambda u: body(u // halves, u % halves))

    each_half(lambda f, h: load(f, h).start())

    barrier = pltpu.get_barrier_semaphore()
    sides = (
        (has_above, dict(sa=gz + 1)), (has_below, dict(sa=gz - 1)),
        (has_up, dict(gy=gy + 1)), (has_down, dict(gy=gy - 1)),
        (has_right, dict(gx=gx + 1)), (has_left, dict(gx=gx - 1)),
    )
    for there, where in sides:
        @pl.when(there)
        def _():
            pl.semaphore_signal(barrier, inc=1, device_id=where, device_id_type=MESH)
    pl.semaphore_wait(barrier, sum(there.astype(jnp.int32) for there, _ in sides))

    def push_x(f, slab, h):
        pl.when(has_left)(lambda: x_left(0, f, slab, h).start())

    def push(f, slab, h):
        pl.when(has_down)(lambda: y_down(f, slab, h).start())
        pl.when(has_up)(lambda: y_up(f, slab, h).start())
        push_x(f, slab, h)

    def halo_y(f, slab, h):
        @pl.when(has_up)
        def _():
            y_down(f, slab, h).wait_recv()
            pl.when(has_left)(lambda: x_left(1, f, slab, h).start())

        @pl.when(has_down)
        def _():
            y_up(f, slab, h).wait_recv()
            pl.when(has_left)(lambda: x_left(2, f, slab, h).start())

    def halo_x(f, slab, h):
        @pl.when(has_right)
        def _():
            x_left(0, f, slab, h).wait_recv()
            pl.when(has_up)(lambda: x_left(1, f, slab, h).wait_recv())
            pl.when(has_down)(lambda: x_left(2, f, slab, h).wait_recv())

    def send_own(u):
        f, v = u // halves, u % halves
        pl.when(raw_up)(lambda: z_up(f, gz, 1 - v).start())
        pl.when(raw_down)(lambda: z_down(f, gz, v).start())

    mine = gz * width // lanes
    row_at = pl.multiple_of(gz * width % lanes, width)
    row_beyond = pl.multiple_of(beside_end * width % lanes, width)

    def products(f, slab, h, both):
        rows = 4 * width if both else 2 * width
        for tx in range(tiles_x):
            for ty in range(tiles_y):
                for part in range(2):
                    turned[part] = own[f, slab, mine, tx, ty, part].T
                for base, start in ((0, row_at), (2 * width, row_beyond))[: 2 if both else 1]:
                    real = turned[0, pl.ds(start, width), :]
                    imag = turned[1, pl.ds(start, width), :]
                    left[base : base + width, :traces] = real
                    left[base : base + width, traces:] = imag
                    left[base + width : base + 2 * width, :traces] = -imag
                    left[base + width : base + 2 * width, traces:] = real
                def tile(ox, oy):
                    if ox == tiles_x:
                        return right.at[f, slab, h, oy + 1]
                    if oy == tiles_y:
                        return up.at[f, slab, h, ox]
                    if oy < 0:
                        return down.at[f, slab, h, ox]
                    return own.at[f, slab, h, ox, oy]

                def add(group):
                    beside = [
                        tile(tx + CANDIDATES[c][0], ty + CANDIDATES[c][1])[...].reshape(2 * traces, lanes)
                        for c in group
                    ]
                    blocks = jnp.dot(
                        left[:rows], jnp.concatenate(beside, axis=1) if len(group) > 1 else beside[0],
                        preferred_element_type=jnp.float32,
                    )
                    for i, c in enumerate(group):
                        block = blocks[:, i * lanes : (i + 1) * lanes]
                        total[f, tx, ty, c, h, :, :lanes] += block[:width]
                        total[f, tx, ty, c, h, :, lanes:] += block[width : 2 * width]
                        if both:
                            beyond[f, tx, ty, c, h, :, :lanes] += block[2 * width : 3 * width]
                            beyond[f, tx, ty, c, h, :, lanes:] += block[3 * width :]

                def run(group, there):
                    if there is True:
                        add(group)
                    else:
                        pl.when(there)(lambda: add(group))

                for group in GROUPS:
                    oy = ty + CANDIDATES[group[0]][1]
                    there = has_up if oy == tiles_y else has_down if oy < 0 else True
                    if tx + 1 < tiles_x:
                        run(group, there)
                        continue
                    near_ones = tuple(c for c in group if CANDIDATES[c][0] == 0)
                    run(group, has_right if there is True else there & has_right)
                    if near_ones:
                        alone = jnp.logical_not(has_right)
                        run(near_ones, alone if there is True else there & alone)

    def choose(f, h, source, target, add):
        for k in range(pairs):
            wanted = offsets[1, k] + 3 * offsets[0, k]
            for tx in range(tiles_x):
                for ty in range(tiles_y):
                    for part in range(2):
                        columns = pl.ds(pl.multiple_of(part * points + h * lanes, lanes), lanes)
                        value = source[f, tx, ty, wanted, h, :, part * lanes : (part + 1) * lanes]
                        if add:
                            value = value + target[tx, ty, k, f, :, columns]
                        target[tx, ty, k, f, :, columns] = value

    def rest(f, slab):
        each(halves, lambda h: halo_y(f, slab, h))

        def part(h):
            halo_x(f, slab, h)
            products(f, slab, h, False)

        each(halves, part)

    each(halves, lambda h: load(0, h).wait())
    send_own(0)

    @pl.when(near)
    def _():
        push(0, gz, jnp.where(near_top, 1, 0))

    each(phases, lambda u: load(u // halves, u % halves).wait(), halves)

    @pl.when(at_end)
    def _():
        send_own(1)
        each_half(lambda f, v: push(f, gz, jnp.where(gz == 0, v, 1 - v)))
        total[...] = jnp.zeros_like(total)

        def pass_halo(f, v):
            h = jnp.where(gz == 0, v, 1 - v)
            halo_y(f, gz, h)
            pl.when(has_up)(lambda: halo_up(f, h).start())
            pl.when(has_down)(lambda: halo_down(f, h).start())
            u = f * halves + v
            pl.when(u + 2 < phases)(lambda: send_own(u + 2))

        each_half(pass_halo)

        def own_part(f, h):
            halo_x(f, gz, h)
            products(f, gz, h, False)

        each_half(own_part)

        def receive(f, v):
            h = jnp.where(gz == 0, v, 1 - v)
            for part in range(2):
                to_end(f, h, part).wait_recv()
            choose(f, h, total, out, True)

        each_half(receive)

    @pl.when(near)
    def _():
        end = beside_end

        def pass_end(u):
            f, v = u // halves, u % halves

            @pl.when(near_top)
            def _():
                z_down(f, end, v).wait_recv()
                z_down(f, end, v).start()
                push_x(f, end, v)

            @pl.when(near_bottom)
            def _():
                z_up(f, end, 1 - v).wait_recv()
                z_up(f, end, 1 - v).start()
                push_x(f, end, 1 - v)

            pl.when(u + 1 < phases)(lambda: send_own(u + 1))

        total[...] = jnp.zeros_like(total)
        beyond[...] = jnp.zeros_like(beyond)

        def near_half(v):
            return jnp.where(near_top, 1 - v, v)

        def work(f, slab, h):
            halo_x(f, slab, h)
            products(f, slab, h, True)

        halo_y(0, gz, near_half(0))
        work(0, gz, near_half(0))
        pass_end(0)

        def rest_half(f, v):
            h = jnp.where(near_top, v, 1 - v)
            halo_y(f, end, h)
            halo_x(f, end, h)
            products(f, end, h, False)

        def phase(f, v):
            u = f * halves + v
            more = u + 1 < phases
            h = near_half(v)
            next_f, next_h = (u + 1) // halves, near_half((u + 1) % halves)

            def at(d):
                slab = jnp.where(near_top, gz - d, gz + d)

                @pl.when(near_top)
                def _():
                    z_up(f, slab, h).wait_recv()

                @pl.when(near_bottom)
                def _():
                    z_down(f, slab, h).wait_recv()

                push(f, slab, h)
                pl.when((d == 1) & more)(lambda: push(next_f, gz, next_h))
                pl.when((d == 2) & more)(lambda: pass_end(u + 1))
                pl.when((d == 1) & (f > 0))(lambda: rest_half(f - 1, v))
                first = jnp.where((d == 2) & more, 0, 1)

                def one(i):
                    own_turn = i == 0
                    pl.when(i == 1)(lambda: halo_y(f, slab, h))
                    work(
                        jnp.where(own_turn, next_f, f),
                        jnp.where(own_turn, gz, slab),
                        jnp.where(own_turn, next_h, h),
                    )

                each(2, one, first)
                pl.when((d == 1) & more)(lambda: halo_y(next_f, gz, next_h))

            each(nz - 1, at, 1)
            choose(f, h, beyond, stage, False)
            for part in range(2):
                to_end(f, h, part).start()

            @pl.when((v == halves - 1) & (f > 0))
            def _():
                each(halves, lambda i: choose(f - 1, i, total, out, False))

        each_half(phase)
        each(halves, lambda v: rest_half(freqs - 1, v))
        each(halves, lambda h: choose(freqs - 1, h, total, out, False))

    if nz > 4:
        @pl.when(middle)
        def _():
            each_half(lambda f, h: push(f, gz, h))
            total[...] = jnp.zeros_like(total)

            def phase(f, v):
                u = f * halves + v

                def at(d):
                    lower, upper = gz - d, gz + d

                    @pl.when(lower >= 0)
                    def _():
                        z_up(f, lower, 1 - v).wait_recv()
                        z_up(f, lower, 1 - v).start()
                        push(f, lower, 1 - v)

                    @pl.when(upper < nz)
                    def _():
                        z_down(f, upper, v).wait_recv()
                        z_down(f, upper, v).start()
                        push(f, upper, v)

                    pl.when((d == 1) & (u + 1 < phases))(lambda: send_own(u + 1))

                each(nz, at, 1)

                @pl.when(v == halves - 1)
                def _():
                    each(nz, lambda slab: rest(f, slab))
                    each(halves, lambda h: choose(f, h, total, out, False))

            each_half(phase)

    def finish(slab):
        def body(f, h):
            pl.when(raw_up & (slab <= gz))(lambda: z_up(f, slab, h).wait_send())
            pl.when(raw_down & (slab >= gz))(lambda: z_down(f, slab, h).wait_send())

            @pl.when(middle | (slab == gz) | (near & (slab != beside_end)))
            def _():
                pl.when(has_down)(lambda: y_down(f, slab, h).wait_send())
                pl.when(has_up)(lambda: y_up(f, slab, h).wait_send())

            @pl.when(at_end & (slab == gz))
            def _():
                pl.when(has_up)(lambda: halo_up(f, h).wait_send())
                pl.when(has_down)(lambda: halo_down(f, h).wait_send())

            @pl.when(inside | (slab == gz))
            def _():

                @pl.when(has_left)
                def _():
                    x_left(0, f, slab, h).wait_send()
                    pl.when(has_up)(lambda: x_left(1, f, slab, h).wait_send())
                    pl.when(has_down)(lambda: x_left(2, f, slab, h).wait_send())

        each_half(body)

    each(nz, finish)

    @pl.when(near)
    def _():
        def body(f, h):
            for part in range(2):
                to_end(f, h, part).wait_send()

        each_half(body)


def hand_on(source, target):
    target[...] = source[...]


def per_device(green, offsets):
    tiles_x, tiles_y, freqs, _, traces, points = green.shape
    nx, ny, nz = (lax.axis_size(name) for name in ("gx", "gy", "sa"))
    width, lanes, pairs = points // nz, 128, offsets.shape[0]
    halves = points // lanes
    dma = pltpu.SemaphoreType.DMA
    result = (tiles_x, tiles_y, pairs, freqs, width, 2 * points)
    sums = (freqs, tiles_x, tiles_y, len(CANDIDATES), halves, width, 2 * lanes)
    piece, cell = (freqs, nz, halves), (2, traces, lanes)
    blocks = pl.pallas_call(
        functools.partial(kernel, nx, ny, nz),
        out_shape=jax.ShapeDtypeStruct(result, jnp.float32),
        in_specs=[pl.BlockSpec(memory_space=pl.ANY), pl.BlockSpec(memory_space=pltpu.SMEM)],
        out_specs=pl.BlockSpec(memory_space=pltpu.VMEM),
        scratch_shapes=[
            pltpu.VMEM(sums, jnp.float32),
            pltpu.VMEM(sums, jnp.float32),
            pltpu.VMEM(result, jnp.float32),
            pltpu.VMEM(piece + (tiles_x, tiles_y) + cell, jnp.bfloat16),
            pltpu.VMEM(piece + (tiles_x,) + cell, jnp.bfloat16),
            pltpu.VMEM(piece + (tiles_x,) + cell, jnp.bfloat16),
            pltpu.VMEM(piece + (tiles_y + 2,) + cell, jnp.bfloat16),
            pltpu.VMEM((2, lanes, traces), jnp.bfloat16),
            pltpu.VMEM((4 * width, 2 * traces), jnp.bfloat16),
            dma((freqs, halves)),
            dma(piece),
            dma(piece),
            dma(piece),
            dma((3,) + piece),
            dma((freqs, halves, 2)),
            dma(piece),
            dma(piece),
            dma(piece),
            dma(piece),
            dma((3,) + piece),
            dma((freqs, halves, 2)),
            dma((2, freqs, halves)),
        ],
        compiler_params=pltpu.CompilerParams(
            collective_id=0, has_side_effects=True, vmem_limit_bytes=61 * 2**20
        ),
        cost_estimate=pl.CostEstimate(
            flops=2 * tiles_x * tiles_y * freqs * len(CANDIDATES) * width * 2 * points * 2 * traces * nz,
            bytes_accessed=12 * 2**20, transcendentals=0,
        ),
    )(green, offsets.T)
    rows = tiles_x * tiles_y * pairs * freqs * width
    spec = pl.BlockSpec((rows // 8, 2 * points), lambda i: (i, 0))
    return pl.pallas_call(
        hand_on,
        grid=(8,),
        out_shape=jax.ShapeDtypeStruct((rows, 2 * points), jnp.float32),
        in_specs=[spec],
        out_specs=spec,
    )(blocks.reshape(rows, 2 * points)).reshape(result)


def solution(mesh):
    return jax.shard_map(
        per_device,
        mesh=mesh,
        in_specs=(P("gx", "gy", None, None, "sa", None), P()),
        out_specs=P("gx", "gy", None, None, "sa", None),
        check_vma=False,
    )
```
